32 devices in a mesh: section: 8 (over y, x, core), dp: 4 (over z).
Axes of the slice: x: 2, y: 2, z: 4, core: 2. Of those that a mesh axis runs over, the one named last changes fastest.
Arguments:
- feed: bfloat16 [2, 4, 64, 512], P(None, None, 'dp'), may hold values from -6 to 6
- proj_in: bfloat16 [2, 8, 512, 1536], P(None, 'section'), may hold values from -0.25 to 0.25
- proj_out: bfloat16 [2, 8, 1536, 512], P(None, 'section'), may hold values from -0.15625 to 0.15625
Outputs:
- grad_a: float32 [8, 512, 1536], P('section', 'dp')
- grad_b: float32 [8, 1536, 512], P('section', 'dp')
The draws below stay inside these ranges and needn't reach their ends.
All inputs are finite; a program needn't handle non-finite values.
Results may differ from the reference program's by a relative error of at most 0.023.
Values may be sent and summed in bfloat16 or wider, within the bound.
A program may use at most 64 MiB of HBM per device.

```python
import jax
import jax.numpy as jnp
from jax import lax

D = 512
R = 1536
MB = 4
TOKENS = 64
N_SECTION = 8


def block_scale(own_key, extent, shards, low, top_value):
    loudness, own = 1.0, jax.random.fold_in(own_key, 6)
    for dim, parts in shards:
        draws = jnp.exp(jax.random.uniform(jax.random.fold_in(own, dim), (parts,), jnp.float32, low / len(shards), top_value / len(shards)))
        loudness = loudness * jnp.repeat(draws, extent[dim] // parts).reshape([-1 if axis == dim else 1 for axis in range(len(extent))])
    return loudness


def scatter_about(rng, shape, spread, limit, cuts=(), dtype=jnp.bfloat16):
    gain = block_scale(rng, shape, cuts, -0.22, 0.18) if cuts else 1.0
    drawn = jax.random.normal(rng, shape, jnp.float32) * spread * gain
    return jnp.minimum(jnp.maximum(drawn, -limit), limit).astype(dtype)


def setup_inputs(seed: int = 0) -> dict:
    key_of = jax.random.split(jax.random.key(seed), 4)
    feed = scatter_about(key_of[0], (2, MB, TOKENS, D), 1.0, 6.0, ((2, 4),))
    proj_in = scatter_about(key_of[1], (2, N_SECTION, D, R), D ** -0.5, 0.25, ((1, 8),))
    proj_out = scatter_about(key_of[2], (2, N_SECTION, R, D), R ** -0.5, 0.15625, ((1, 8),))
    return {"feed": feed, "proj_in": proj_in, "proj_out": proj_out}


def forward_section(activ, weight_in, weight_out):
    wide = activ.astype(jnp.float32)
    factor = lax.rsqrt(lax.optimization_barrier(jnp.mean(wide * wide, axis=-1, keepdims=True)) + 1e-05)
    normed = (wide * factor).astype(jnp.bfloat16)
    before = jnp.dot(normed, weight_in, preferred_element_type=jnp.float32)
    hidden = (before * jax.nn.sigmoid(before)).astype(jnp.bfloat16)
    result = (wide + jnp.dot(hidden, weight_out, preferred_element_type=jnp.float32)).astype(jnp.bfloat16)
    return (result, before)

def backward_section(activ, before, weight_in, weight_out, incoming):
    wide = activ.astype(jnp.float32)
    factor = lax.rsqrt(lax.optimization_barrier(jnp.mean(wide * wide, axis=-1, keepdims=True)) + 1e-05)
    scaled = wide * factor
    normed = scaled.astype(jnp.bfloat16)
    hidden = (before * jax.nn.sigmoid(before)).astype(jnp.bfloat16)
    d_hidden = jnp.dot(incoming, weight_out.T, preferred_element_type=jnp.float32)
    sigma = jax.nn.sigmoid(before)
    d_before = (d_hidden * sigma * (1.0 + before * (1.0 - sigma))).astype(jnp.bfloat16)
    d_normed = jnp.dot(d_before, weight_in.T, preferred_element_type=jnp.float32)
    outgoing = incoming.astype(jnp.float32) + factor * (d_normed - scaled * lax.optimization_barrier(jnp.mean(d_normed * scaled, axis=-1, keepdims=True)))
    grad_in_t = jnp.dot(d_before.T, normed, preferred_element_type=jnp.float32)
    grad_out = jnp.dot(hidden.T, incoming, preferred_element_type=jnp.float32)
    return (outgoing.astype(jnp.bfloat16), grad_in_t, grad_out)

def reference(feed, proj_in, proj_out):
    seed_scale = 8.0 / (MB * TOKENS)
    acc_in = [jnp.zeros((R, D), jnp.float32) for section_index in range(N_SECTION)]
    acc_out = [jnp.zeros((R, D), jnp.float32) for section_index in range(N_SECTION)]
    for relay in range(2):
        for micro_index in range(MB):
            activ = feed[relay, micro_index]
            saved = []
            for section_index in range(N_SECTION):
                holder = section_index if relay == 0 else N_SECTION - 1 - section_index
                result, before = forward_section(activ, proj_in[relay, holder], proj_out[relay, holder])
                saved.append((activ, before))
                activ = result
            incoming = (seed_scale * activ.astype(jnp.float32)).astype(jnp.bfloat16)
            for section_index in range(N_SECTION - 1, -1, -1):
                holder = section_index if relay == 0 else N_SECTION - 1 - section_index
                kept, before = saved[section_index]
                incoming, term_in, term_out = backward_section(kept, before, proj_in[relay, holder], proj_out[relay, holder], incoming)
                acc_in[section_index] = acc_in[section_index] + term_in
                acc_out[section_index] = acc_out[section_index] + term_out
    grad_a = jnp.stack([jnp.transpose(term) for term in acc_in])
    grad_b = jnp.stack(acc_out)
    return (grad_a, grad_b)
```

```python
import functools

import jax
import jax.numpy as jnp
from jax import lax
from jax.experimental import pallas as pl
from jax.experimental.pallas import tpu as pltpu
from jax.sharding import PartitionSpec as P

MESH = pl.DeviceIdType.MESH
F32, BF16 = jnp.float32, jnp.bfloat16
HOP_CHUNKS = 2
UNIT_CHUNKS = 3


def dot(a, b):
    return jnp.dot(a, b, preferred_element_type=F32)


def dot_nt(a, b):
    return lax.dot_general(a, b, (((1,), (1,)), ((), ())), preferred_element_type=F32)


def norm_factor(wide):
    return lax.rsqrt(jnp.mean(wide * wide, axis=-1, keepdims=True) + 1e-05)


def relay_kernel(
    S, DP, scale,
    feed, win, wout, oa, ob,
    wa, wb, h_all, g_all, h_out, g_out, pre_own, dsl_own, hid_own, dpre_own, u_own, r_own,
    n_t, h_t, dsl_all, up_a, up_b, got_a, got_b, full_t,
    load_sem, feed_sem, hop_send, hop_recv, all_send, all_recv, up_send, up_recv,
):
    s, d = lax.axis_index("section"), lax.axis_index("dp")
    M, D = h_all.shape[2], h_all.shape[3]
    R = wa.shape[2]
    T = DP * M
    ra, rb = D // DP, R // DP
    half = S // 2
    p0 = s // half
    p1 = 1 - p0
    k0 = s + p0 * (S - 1 - 2 * s)
    mirror = S - 1 - s
    cw, uw = D // HOP_CHUNKS, R // UNIT_CHUNKS

    def load(i, src, dst, p):
        return pltpu.make_async_copy(src.at[p, 0], dst.at[p], load_sem.at[i, p])

    feed_copy = pltpu.make_async_copy(feed.at[p0], h_all.at[p0, d], feed_sem)

    @pl.when(k0 == 0)
    def _():
        feed_copy.start()

    for p in (p0, p1):
        load(0, win, wa, p).start()
        load(1, wout, wb, p).start()

    barrier = pltpu.get_barrier_semaphore()
    for other in (lax.rem(s + 1, S), lax.rem(s + S - 1, S), mirror):
        pl.semaphore_signal(barrier, inc=1, device_id={"section": other}, device_id_type=MESH)
    for o in range(1, DP):
        pl.semaphore_signal(
            barrier, inc=1, device_id={"dp": lax.rem(d + o, DP)}, device_id_type=MESH
        )
    pl.semaphore_wait(barrier, 3 + DP - 1)

    def hop(kind, p, c):
        step = 1 - 2 * p
        peer = s + step if kind == 0 else s - step
        src, dst = (h_out, h_all) if kind == 0 else (g_out, g_all)
        cols = pl.ds(c * cw, cw)
        return pltpu.make_async_remote_copy(
            src_ref=src.at[p, :, cols],
            dst_ref=dst.at[p, d, :, cols],
            send_sem=hop_send.at[kind, p, c],
            recv_sem=hop_recv.at[kind, p, c],
            device_id={"section": peer},
            device_id_type=MESH,
        )

    def share(kind, p, o):
        buf = h_all if kind == 0 else g_all
        return pltpu.make_async_remote_copy(
            src_ref=buf.at[p, d],
            dst_ref=buf.at[p, d],
            send_sem=all_send.at[kind, p, o - 1],
            recv_sem=all_recv.at[kind, p, o - 1],
            device_id={"dp": lax.rem(d + o, DP)},
            device_id_type=MESH,
        )

    def take(kind, p, o):
        buf = h_all if kind == 0 else g_all
        source = lax.rem(d + DP - o, DP)
        return pltpu.make_async_remote_copy(
            src_ref=buf.at[p, source],
            dst_ref=buf.at[p, source],
            send_sem=all_send.at[kind, p, o - 1],
            recv_sem=all_recv.at[kind, p, o - 1],
            device_id={"dp": source},
            device_id_type=MESH,
        )

    def share_start(kind, p):
        for o in range(1, DP):
            share(kind, p, o).start()

    def take_wait(kind, p):
        for o in range(1, DP):
            take(kind, p, o).wait_recv()

    def up_copy(i):
        src, dst = ((up_b, got_b), (up_a, got_a))[min(i, 1)]
        if i:
            cols = pl.ds((i - 1) * uw, uw)
            src, dst = src.at[:, cols], dst.at[:, cols]
        return pltpu.make_async_remote_copy(
            src_ref=src,
            dst_ref=dst,
            send_sem=up_send.at[i],
            recv_sem=up_recv.at[i],
            device_id={"section": mirror},
            device_id_type=MESH,
        )

    def forward(p, sends):
        wide = h_all[p, d].astype(F32)
        factor = norm_factor(wide)
        scaled = wide * factor
        normed = scaled.astype(BF16)
        for c in range(UNIT_CHUNKS):
            cols = pl.ds(c * uw, uw)
            before = dot(normed, wa[p, :, cols])
            hid_own[:, cols] = (before * jax.nn.sigmoid(before)).astype(BF16)
            pre_own[p, :, cols] = before
        for c in range(HOP_CHUNKS):
            cols = pl.ds(c * cw, cw)
            old = h_all[p, d, :, cols].astype(F32)
            h_out[p, :, cols] = (old + dot(hid_own[...], wb[p, :, cols])).astype(BF16)

            @pl.when(sends)
            def _():
                hop(0, p, c).start()

        share_start(0, p)
        u_own[p] = scaled
        r_own[p] = jnp.broadcast_to(factor, (M, 128))
        for c in range(UNIT_CHUNKS):
            cols = pl.ds(c * uw, uw)
            before = pre_own[p, :, cols]
            sigma = jax.nn.sigmoid(before)
            dsl_own[p, :, cols] = sigma * (1.0 + before * (1.0 - sigma))

    def backward(p):
        incoming = g_all[p, d]
        total = jnp.zeros((M, 1), F32)
        for c in range(UNIT_CHUNKS):
            cols = pl.ds(c * uw, uw)
            d_hidden = dot_nt(incoming, wb[p, cols, :])
            d_before = (d_hidden * dsl_own[p, :, cols]).astype(BF16)
            dpre_own[:, cols] = d_before
            total += jnp.sum(
                d_before.astype(F32) * pre_own[p, :, cols], axis=-1, keepdims=True
            )
        mean = total * (1.0 / D)
        factor = r_own[p, :, 0:1]
        for c in range(HOP_CHUNKS):
            cols = pl.ds(c * cw, cw)
            d_normed = dot_nt(dpre_own[...], wa[p, cols, :])
            out = g_all[p, d, :, cols].astype(F32) + factor * (
                d_normed - u_own[p, :, cols] * mean
            )
            g_out[p, :, cols] = out.astype(BF16)
            hop(1, p, c).start()

    aligned = ra % 128 == 0 and rb % 128 == 0
    block = min(T, 256)

    def prepare(p):
        take_wait(0, p)

        def rows_step(b):
            per = block // M
            rows = pl.ds(pl.multiple_of(b * block, block), block)
            wide = h_all[p, pl.ds(b * per, per)].reshape(block, D).astype(F32)
            normed_wide = wide * norm_factor(wide)
            normed = normed_wide.astype(BF16)
            if aligned:
                mine = h_all[
                    p, pl.ds(b * per, per), :, pl.ds(pl.multiple_of(d * ra, 128), ra)
                ].reshape(block, ra).astype(F32) * norm_factor(wide)
                n_t[p, :, rows] = mine.T.astype(BF16)
            else:
                full_t[0:D, rows] = normed_wide.T.astype(BF16)
            for c in range(UNIT_CHUNKS):
                cols = pl.ds(c * uw, uw)
                before = dot(normed, wa[p, :, cols])
                sigma = jax.nn.sigmoid(before)
                hidden = before * sigma
                dsl_all[p, rows, cols] = sigma * (1.0 + before * (1.0 - sigma))
                if not aligned:
                    full_t[D + c * uw:D + (c + 1) * uw, rows] = hidden.T.astype(BF16)
            if aligned:
                before = dot(normed, wa[p, :, pl.ds(pl.multiple_of(d * rb, 128), rb)])
                hidden = before * jax.nn.sigmoid(before)
                h_t[p, :, rows] = hidden.T.astype(BF16)

        if T == block:
            rows_step(0)
        else:
            pl.loop(0, T // block)(rows_step)
        if not aligned:
            n_t[p] = full_t[pl.ds(pl.multiple_of(d * ra, 16), ra), :]
            h_t[p] = full_t[pl.ds(pl.multiple_of(D + d * rb, 16), rb), :]

    def gradients(p):
        take_wait(1, p)
        gs = g_all[p].reshape(T, D)
        term = dot(h_t[p], gs)

        @pl.when(p == 1)
        def _():
            up_b[...] = term.astype(BF16)
            up_copy(0).start()

        @pl.when(p == 0)
        def _():
            ob[0] = term

        for c in range(UNIT_CHUNKS):
            cols = pl.ds(c * uw, uw)
            d_hidden = dot_nt(gs, wb[p, cols, :])
            d_before = (d_hidden * dsl_all[p, :, cols]).astype(BF16)
            term = dot(n_t[p], d_before)

            @pl.when(p == 1)
            def _():
                up_a[:, cols] = term.astype(BF16)
                up_copy(1 + c).start()

            @pl.when(p == 0)
            def _():
                oa[0, :, cols] = term

    early = k0 < S // 4

    load(0, win, wa, p0).wait()
    load(1, wout, wb, p0).wait()

    @pl.when(k0 == 0)
    def _():
        feed_copy.wait()

    @pl.when(k0 > 0)
    def _():
        for c in range(HOP_CHUNKS):
            hop(0, p0, c).wait_recv()

    forward(p0, k0 < S)

    load(0, win, wa, p1).wait()
    load(1, wout, wb, p1).wait()

    @pl.when(early)
    def _():
        prepare(p0)

    for c in range(HOP_CHUNKS):
        hop(0, p1, c).wait_recv()
    forward(p1, k0 > 0)

    @pl.when(k0 >= S // 4)
    def _():
        prepare(p0)
        prepare(p1)

    @pl.when(k0 == 0)
    def _():
        g_all[p1, d] = (scale * h_out[p1].astype(F32)).astype(BF16)

    @pl.when(k0 > 0)
    def _():
        for c in range(HOP_CHUNKS):
            hop(1, p1, c).wait_recv()

    backward(p1)
    share_start(1, p1)

    @pl.when(early)
    def _():
        prepare(p1)

    @pl.when(k0 < half - 1)
    def _():
        gradients(p1)

    for c in range(HOP_CHUNKS):
        hop(1, p0, c).wait_recv()

    @pl.when(k0 > 0)
    def _():
        backward(p0)

    share_start(1, p0)

    @pl.when(k0 == half - 1)
    def _():
        gradients(p1)

    gradients(p0)

    up_copy(0).wait_recv()
    ob[0] = ob[0] + got_b[...].astype(F32)
    for c in range(UNIT_CHUNKS):
        cols = pl.ds(c * uw, uw)
        up_copy(1 + c).wait_recv()
        oa[0, :, cols] = oa[0, :, cols] + got_a[:, cols].astype(F32)

    for c in range(HOP_CHUNKS):
        hop(0, p0, c).wait_send()
        hop(1, p1, c).wait_send()

    @pl.when(k0 > 0)
    def _():
        for c in range(HOP_CHUNKS):
            hop(0, p1, c).wait_send()
            hop(1, p0, c).wait_send()

    for kind in range(2):
        for p in (p0, p1):
            for o in range(1, DP):
                share(kind, p, o).wait_send()
    for i in range(1 + UNIT_CHUNKS):
        up_copy(i).wait_send()


def per_device(feed, proj_in, proj_out):
    S, DP = lax.axis_size("section"), lax.axis_size("dp")
    micro, rows, D = feed.shape[1:]
    R = proj_in.shape[3]
    M, T = micro * rows, micro * rows * DP
    ra, rb = D // DP, R // DP
    scale = 8.0 / T
    aligned = ra % 128 == 0 and rb % 128 == 0
    vm = pltpu.VMEM
    dma = pltpu.SemaphoreType.DMA
    peers = max(DP - 1, 1)
    return pl.pallas_call(
        functools.partial(relay_kernel, S, DP, scale),
        out_shape=(
            jax.ShapeDtypeStruct((1, ra, R), F32),
            jax.ShapeDtypeStruct((1, rb, D), F32),
        ),
        in_specs=[pl.BlockSpec(memory_space=pl.ANY)] * 3,
        out_specs=(pl.BlockSpec(memory_space=pltpu.VMEM),) * 2,
        scratch_shapes=[
            vm((2, D, R), BF16),
            vm((2, R, D), BF16),
            vm((2, DP, M, D), BF16),
            vm((2, DP, M, D), BF16),
            vm((2, M, D), BF16),
            vm((2, M, D), BF16),
            vm((2, M, R), F32),
            vm((2, M, R), F32),
            vm((M, R), BF16),
            vm((M, R), BF16),
            vm((2, M, D), F32),
            vm((2, M, 128), F32),
            vm((2, ra, T), BF16),
            vm((2, rb, T), BF16),
            vm((2, T, R), F32),
            vm((ra, R), BF16),
            vm((rb, D), BF16),
            vm((ra, R), BF16),
            vm((rb, D), BF16),
            vm((16, 128) if aligned else (D + R, T), BF16),
            dma((2, 2)),
            dma(()),
            dma((2, 2, HOP_CHUNKS)),
            dma((2, 2, HOP_CHUNKS)),
            dma((2, 2, peers)),
            dma((2, 2, peers)),
            dma((1 + UNIT_CHUNKS,)),
            dma((1 + UNIT_CHUNKS,)),
        ],
        compiler_params=pltpu.CompilerParams(
            collective_id=0, has_side_effects=True, vmem_limit_bytes=60 * 1024 * 1024
        ),
        cost_estimate=pl.CostEstimate(
            flops=40 * M * D * R, bytes_accessed=16 * D * R, transcendentals=8 * T * R
        ),
    )(feed.reshape(2, M, D), proj_in, proj_out)


def solution(mesh):
    in_specs = (
        P(None, None, "dp", None),
        P(None, "section", None, None),
        P(None, "section", None, None),
    )
    out_specs = (P("section", "dp", None), P("section", "dp", None))
    return jax.shard_map(
        per_device, mesh=mesh, in_specs=in_specs, out_specs=out_specs, check_vma=False
    )
```

```python
import functools

import jax
import jax.numpy as jnp
from jax import lax
from jax.experimental import pallas as pl
from jax.experimental.pallas import tpu as pltpu
from jax.sharding import PartitionSpec as P

MESH = pl.DeviceIdType.MESH
F32, BF16 = jnp.float32, jnp.bfloat16
HOP_CHUNKS = 2
UNIT_CHUNKS = 3


def dot(a, b):
    return jnp.dot(a, b, preferred_element_type=F32)


def dot_nt(a, b):
    return lax.dot_general(a, b, (((1,), (1,)), ((), ())), preferred_element_type=F32)


def sigmoid(x):
    return 0.5 + 0.5 * jnp.tanh(0.5 * x)


def norm_factor(wide):
    return lax.rsqrt(jnp.mean(wide * wide, axis=-1, keepdims=True) + 1e-05)


def relay_kernel(
    S, DP, scale,
    feed, win, wout, oa, ob,
    wa, wb, h_all, g_all, h_out, g_out, pre_own, dsl_own, hid_own, dpre_own, u_own, r_own,
    n_t, h_t, dsl_all, up_a, up_b, got_a, got_b, own_a, own_b, dh_own, full_t,
    load_sem, feed_sem, hop_send, hop_recv, all_send, all_recv, up_send, up_recv,
):
    s, d = lax.axis_index("section"), lax.axis_index("dp")
    M, D = h_all.shape[2], h_all.shape[3]
    R = wa.shape[2]
    T = DP * M
    ra, rb = D // DP, R // DP
    half = S // 2
    p0 = s // half
    p1 = 1 - p0
    k0 = s + p0 * (S - 1 - 2 * s)
    mirror = S - 1 - s
    cw, uw = D // HOP_CHUNKS, R // UNIT_CHUNKS

    def unit_cols(c):
        return pl.ds(pl.multiple_of(c * uw, uw), uw)

    def load(i, src, dst, p):
        return pltpu.make_async_copy(src.at[p, 0], dst.at[p], load_sem.at[i, p])

    feed_copy = pltpu.make_async_copy(feed.at[p0], h_all.at[p0, d], feed_sem)

    @pl.when(k0 == 0)
    def _():
        feed_copy.start()

    for p in (p0, p1):
        load(0, win, wa, p).start()
        load(1, wout, wb, p).start()

    barrier = pltpu.get_barrier_semaphore()
    for other in (lax.rem(s + 1, S), lax.rem(s + S - 1, S), mirror):
        pl.semaphore_signal(barrier, inc=1, device_id={"section": other}, device_id_type=MESH)
    for o in range(1, DP):
        pl.semaphore_signal(
            barrier, inc=1, device_id={"dp": lax.rem(d + o, DP)}, device_id_type=MESH
        )
    pl.semaphore_wait(barrier, 3 + DP - 1)

    def hop(kind, p, c):
        step = 1 - 2 * p
        peer = s + step if kind == 0 else s - step
        src, dst = (h_out, h_all) if kind == 0 else (g_out, g_all)
        cols = pl.ds(c * cw, cw)
        return pltpu.make_async_remote_copy(
            src_ref=src.at[p, :, cols],
            dst_ref=dst.at[p, d, :, cols],
            send_sem=hop_send.at[kind, p, c],
            recv_sem=hop_recv.at[kind, p, c],
            device_id={"section": peer},
            device_id_type=MESH,
        )

    def share(kind, p, o):
        buf = h_all if kind == 0 else g_all
        return pltpu.make_async_remote_copy(
            src_ref=buf.at[p, d],
            dst_ref=buf.at[p, d],
            send_sem=all_send.at[kind, p, o - 1],
            recv_sem=all_recv.at[kind, p, o - 1],
            device_id={"dp": lax.rem(d + o, DP)},
            device_id_type=MESH,
        )

    def take(kind, p, o):
        buf = h_all if kind == 0 else g_all
        source = lax.rem(d + DP - o, DP)
        return pltpu.make_async_remote_copy(
            src_ref=buf.at[p, source],
            dst_ref=buf.at[p, source],
            send_sem=all_send.at[kind, p, o - 1],
            recv_sem=all_recv.at[kind, p, o - 1],
            device_id={"dp": source},
            device_id_type=MESH,
        )

    def share_start(kind, p):
        for o in range(1, DP):
            share(kind, p, o).start()

    def take_wait(kind, p):
        for o in range(1, DP):
            take(kind, p, o).wait_recv()

    def up_copy_b():
        return pltpu.make_async_remote_copy(
            src_ref=up_b,
            dst_ref=got_b,
            send_sem=up_send.at[0],
            recv_sem=up_recv.at[0],
            device_id={"section": mirror},
            device_id_type=MESH,
        )

    def up_copy_a(c):
        cols = unit_cols(c)
        return pltpu.make_async_remote_copy(
            src_ref=up_a.at[:, cols],
            dst_ref=got_a.at[:, cols],
            send_sem=up_send.at[1 + c],
            recv_sem=up_recv.at[1 + c],
            device_id={"section": mirror},
            device_id_type=MESH,
        )

    def forward(p, k):
        load(0, win, wa, p).wait()

        @pl.when(k == 0)
        def _():
            feed_copy.wait()

        squares = jnp.zeros((M, 1), F32)
        for c in range(HOP_CHUNKS):
            part = pl.ds(c * cw, cw)

            @pl.when(k > 0)
            def _():
                hop(0, p, c).wait_recv()

            piece = h_all[p, d, :, part]
            wide = piece.astype(F32)
            squares += jnp.sum(wide * wide, axis=-1, keepdims=True)
            last = c == HOP_CHUNKS - 1
            if last:
                factor = lax.rsqrt(squares * (1.0 / D) + 1e-05)
            for u in range(UNIT_CHUNKS):
                cols = pl.ds(u * uw, uw)
                before = dot(piece, wa[p, part, cols])
                if c:
                    before += pre_own[p, :, cols]
                if last:
                    before *= factor
                    hid_own[:, cols] = (before * sigmoid(before)).astype(BF16)
                pre_own[p, :, cols] = before
        load(1, wout, wb, p).wait()
        for c in range(HOP_CHUNKS):
            cols = pl.ds(c * cw, cw)
            old = h_all[p, d, :, cols].astype(F32)
            h_out[p, :, cols] = (old + dot(hid_own[...], wb[p, :, cols])).astype(BF16)

            @pl.when(k < S - 1)
            def _():
                hop(0, p, c).start()

        share_start(0, p)
        u_own[p] = h_all[p, d].astype(F32) * factor
        r_own[p] = jnp.broadcast_to(factor, (M, 128))
        for u in range(UNIT_CHUNKS):
            cols = pl.ds(u * uw, uw)
            before = pre_own[p, :, cols]
            sigma = sigmoid(before)
            dsl_own[p, :, cols] = sigma * (1.0 + before * (1.0 - sigma))

    def backward(p, k):
        @pl.when(k == S - 1)
        def _():
            g_all[p, d] = (scale * h_out[p].astype(F32)).astype(BF16)

        @pl.when(k == 0)
        def _():
            for c in range(HOP_CHUNKS):
                hop(1, p, c).wait_recv()
            share_start(1, p)

        @pl.when(k > 0)
        def _():
            total = jnp.zeros((M, 1), F32)
            for c in range(HOP_CHUNKS):
                part = pl.ds(c * cw, cw)

                @pl.when(k < S - 1)
                def _():
                    hop(1, p, c).wait_recv()

                piece = g_all[p, d, :, part]
                for u in range(UNIT_CHUNKS):
                    cols = pl.ds(u * uw, uw)
                    d_hidden = dot_nt(piece, wb[p, cols, part])
                    if c:
                        d_hidden += dh_own[:, cols]
                    if c < HOP_CHUNKS - 1:
                        dh_own[:, cols] = d_hidden
                    else:
                        d_before = (d_hidden * dsl_own[p, :, cols]).astype(BF16)
                        dpre_own[:, cols] = d_before
                        total += jnp.sum(
                            d_before.astype(F32) * pre_own[p, :, cols], axis=-1, keepdims=True
                        )
            mean = total * (1.0 / D)
            factor = r_own[p, :, 0:1]
            for c in range(HOP_CHUNKS):
                cols = pl.ds(c * cw, cw)
                d_normed = dot_nt(dpre_own[...], wa[p, cols, :])
                out = g_all[p, d, :, cols].astype(F32) + factor * (
                    d_normed - u_own[p, :, cols] * mean
                )
                g_out[p, :, cols] = out.astype(BF16)
                hop(1, p, c).start()
            share_start(1, p)

    aligned = ra % 128 == 0 and rb % 128 == 0
    block = min(T, 256)

    def prepare(p):
        take_wait(0, p)

        def rows_step(b):
            per = block // M
            rows = pl.ds(pl.multiple_of(b * block, block), block)
            wide = h_all[p, pl.ds(b * per, per)].reshape(block, D).astype(F32)
            factor = norm_factor(wide)
            normed_wide = wide * factor
            normed = normed_wide.astype(BF16)
            if aligned:
                mine = h_all[
                    p, pl.ds(b * per, per), :, pl.ds(pl.multiple_of(d * ra, 128), ra)
                ].reshape(block, ra).astype(F32) * factor
                n_t[p, :, rows] = mine.T.astype(BF16)
                before = dot(normed, wa[p, :, pl.ds(pl.multiple_of(d * rb, 128), rb)])
                h_t[p, :, rows] = (before * sigmoid(before)).T.astype(BF16)
            else:
                full_t[0:D, rows] = normed_wide.T.astype(BF16)

            @pl.loop(0, UNIT_CHUNKS)
            def _(c):
                cols = unit_cols(c)
                before = dot(normed, wa[p, :, cols])
                sigma = sigmoid(before)
                dsl_all[p, rows, cols] = sigma * (1.0 + before * (1.0 - sigma))
                if not aligned:
                    full_t[pl.ds(pl.multiple_of(D + c * uw, 16), uw), rows] = (
                        (before * sigma).T.astype(BF16)
                    )

        if T == block:
            rows_step(0)
        else:
            pl.loop(0, T // block)(rows_step)
        if not aligned:
            n_t[p] = full_t[pl.ds(pl.multiple_of(d * ra, 16), ra), :]
            h_t[p] = full_t[pl.ds(pl.multiple_of(D + d * rb, 16), rb), :]

    def gradients(p):
        take_wait(1, p)
        gs = g_all[p].reshape(T, D)
        term = dot(h_t[p], gs)

        @pl.when(p == 1)
        def _():
            up_b[...] = term.astype(BF16)
            up_copy_b().start()

        @pl.when(p == 0)
        def _():
            own_b[...] = term

        @pl.loop(0, UNIT_CHUNKS)
        def _(c):
            cols = unit_cols(c)
            d_hidden = dot_nt(g_all[p].reshape(T, D), wb[p, cols, :])
            d_before = (d_hidden * dsl_all[p, :, cols]).astype(BF16)
            term = dot(n_t[p], d_before)

            @pl.when(p == 1)
            def _():
                up_a[:, cols] = term.astype(BF16)
                up_copy_a(c).start()

            @pl.when(p == 0)
            def _():
                own_a[:, cols] = term

    early = (k0 < S // 4).astype(jnp.int32)
    middle = (k0 == half - 1).astype(jnp.int32)

    @pl.loop(0, 4)
    def _(j):
        q = lax.rem((j + 1) // 2, 2)
        p = p0 + q * (1 - 2 * p0)
        k = k0 + q * (S - 1 - 2 * k0)

        @pl.when(j < 2)
        def _():
            forward(p, k)

        @pl.when(j >= 2)
        def _():
            backward(p, k)

        is1 = (j == 1).astype(jnp.int32)
        is2 = (j == 2).astype(jnp.int32)
        is3 = (j == 3).astype(jnp.int32)
        first = early * is2
        count = early * (1 - is1 - is3) + (1 - early) * 2 * is1

        @pl.loop(0, count)
        def _(i):
            prepare(p0 + (first + i) * (1 - 2 * p0))

        count = is2 * (1 - middle) + is3 * (1 + middle)

        @pl.loop(0, count)
        def _(i):
            which = is2 + is3 * (middle - i)
            gradients(p0 + which * (1 - 2 * p0))

    up_copy_b().wait_recv()
    ob[...] = (own_b[...] + got_b[...].astype(F32)).astype(BF16)
    for c in range(UNIT_CHUNKS):
        cols = pl.ds(c * uw, uw)
        up_copy_a(c).wait_recv()
        oa[:, cols] = (own_a[:, cols] + got_a[:, cols].astype(F32)).astype(BF16)

    for c in range(HOP_CHUNKS):
        hop(0, p0, c).wait_send()
        hop(1, p1, c).wait_send()

    @pl.when(k0 > 0)
    def _():
        for c in range(HOP_CHUNKS):
            hop(0, p1, c).wait_send()
            hop(1, p0, c).wait_send()

    for kind in range(2):
        for p in (p0, p1):
            for o in range(1, DP):
                share(kind, p, o).wait_send()
    up_copy_b().wait_send()
    for c in range(UNIT_CHUNKS):
        up_copy_a(c).wait_send()


def per_device(feed, proj_in, proj_out):
    S, DP = lax.axis_size("section"), lax.axis_size("dp")
    micro, rows, D = feed.shape[1:]
    R = proj_in.shape[3]
    M, T = micro * rows, micro * rows * DP
    ra, rb = D // DP, R // DP
    scale = 8.0 / T
    aligned = ra % 128 == 0 and rb % 128 == 0
    vm = pltpu.VMEM
    dma = pltpu.SemaphoreType.DMA
    peers = max(DP - 1, 1)
    grad_a, grad_b = pl.pallas_call(
        functools.partial(relay_kernel, S, DP, scale),
        out_shape=(
            jax.ShapeDtypeStruct((ra, R), BF16),
            jax.ShapeDtypeStruct((rb, D), BF16),
        ),
        in_specs=[pl.BlockSpec(memory_space=pltpu.HBM)] * 3,
        out_specs=(pl.BlockSpec(memory_space=pltpu.VMEM),) * 2,
        scratch_shapes=[
            vm((2, D, R), BF16),
            vm((2, R, D), BF16),
            vm((2, DP, M, D), BF16),
            vm((2, DP, M, D), BF16),
            vm((2, M, D), BF16),
            vm((2, M, D), BF16),
            vm((2, M, R), F32),
            vm((2, M, R), F32),
            vm((M, R), BF16),
            vm((M, R), BF16),
            vm((2, M, D), F32),
            vm((2, M, 128), F32),
            vm((2, ra, T), BF16),
            vm((2, rb, T), BF16),
            vm((2, T, R), F32),
            vm((ra, R), BF16),
            vm((rb, D), BF16),
            vm((ra, R), BF16),
            vm((rb, D), BF16),
            vm((ra, R), F32),
            vm((rb, D), F32),
            vm((M, R), F32),
            vm((16, 128) if aligned else (D + R, T), BF16),
            dma((2, 2)),
            dma(()),
            dma((2, 2, HOP_CHUNKS)),
            dma((2, 2, HOP_CHUNKS)),
            dma((2, 2, peers)),
            dma((2, 2, peers)),
            dma((1 + UNIT_CHUNKS,)),
            dma((1 + UNIT_CHUNKS,)),
        ],
        compiler_params=pltpu.CompilerParams(
            collective_id=0, has_side_effects=True, vmem_limit_bytes=60 * 1024 * 1024
        ),
        cost_estimate=pl.CostEstimate(
            flops=40 * M * D * R, bytes_accessed=16 * D * R, transcendentals=8 * T * R
        ),
    )(feed.reshape(2, M, D), proj_in, proj_out)
    return grad_a.astype(F32)[None], grad_b.astype(F32)[None]


def solution(mesh):
    in_specs = (
        P(None, None, "dp", None),
        P(None, "section", None, None),
        P(None, "section", None, None),
    )
    out_specs = (P("section", "dp", None), P("section", "dp", None))
    return jax.shard_map(
        per_device, mesh=mesh, in_specs=in_specs, out_specs=out_specs, check_vma=False
    )
```

```python
import functools

import jax
import jax.numpy as jnp
from jax import lax
from jax.experimental import pallas as pl
from jax.experimental.pallas import tpu as pltpu
from jax.sharding import PartitionSpec as P

MESH = pl.DeviceIdType.MESH
F32, BF16 = jnp.float32, jnp.bfloat16
HOP_CHUNKS = 2
UNIT_CHUNKS = 3
GRAD_CHUNKS = 2
PIECES = 4


def dot(a, b):
    return jnp.dot(a, b, preferred_element_type=F32)


def dot_nt(a, b):
    return lax.dot_general(a, b, (((1,), (1,)), ((), ())), preferred_element_type=F32)


def sigmoid(x):
    return 0.5 + 0.5 * jnp.tanh(0.5 * x)


def norm_factor(wide):
    return lax.rsqrt(jnp.mean(wide * wide, axis=-1, keepdims=True) + 1e-05)


def relay_kernel(
    S, DP, scale,
    feed, win, wout, oa, ob,
    wa, wb, h_all, g_all, h_out, g_out, pre_own, dsl_own, hid_own, dpre_own, u_own, r_own,
    n_t, h_t, dsl_all, up_a, up_b, got_a, got_b, own_a, own_b, dh_own, via_a, via_b, full_t,
    load_sem, feed_sem, hop_send, hop_recv, all_send, all_recv, up_send, up_recv, via_send, via_recv,
):
    s, d = lax.axis_index("section"), lax.axis_index("dp")
    M, D = h_all.shape[2], h_all.shape[3]
    R = wa.shape[2]
    T = DP * M
    ra, rb = D // DP, R // DP
    half = S // 2
    p0 = s // half
    p1 = 1 - p0
    k0 = s + p0 * (S - 1 - 2 * s)
    mirror = S - 1 - s
    flip = s + 2 * (1 - 2 * lax.rem(s // 2, 2))
    cross = S - 1 - flip
    cw, uw = D // HOP_CHUNKS, R // UNIT_CHUNKS

    def unit_cols(c):
        return pl.ds(pl.multiple_of(c * uw, uw), uw)

    def load(i, src, dst, p):
        return pltpu.make_async_copy(src.at[p, 0], dst.at[p], load_sem.at[i, p])

    feed_copy = pltpu.make_async_copy(feed.at[p0], h_all.at[p0, d], feed_sem)

    @pl.when(k0 == 0)
    def _():
        feed_copy.start()

    for p in (p0, p1):
        load(0, win, wa, p).start()
        load(1, wout, wb, p).start()

    barrier = pltpu.get_barrier_semaphore()
    for other in (lax.rem(s + 1, S), lax.rem(s + S - 1, S), mirror, flip, cross):
        pl.semaphore_signal(barrier, inc=1, device_id={"section": other}, device_id_type=MESH)
    for o in range(1, DP):
        pl.semaphore_signal(
            barrier, inc=1, device_id={"dp": lax.rem(d + o, DP)}, device_id_type=MESH
        )
    pl.semaphore_wait(barrier, 5 + DP - 1)

    def hop(kind, p, c):
        step = 1 - 2 * p
        peer = s + step if kind == 0 else s - step
        src, dst = (h_out, h_all) if kind == 0 else (g_out, g_all)
        cols = pl.ds(c * cw, cw)
        return pltpu.make_async_remote_copy(
            src_ref=src.at[p, :, cols],
            dst_ref=dst.at[p, d, :, cols],
            send_sem=hop_send.at[kind, p, c],
            recv_sem=hop_recv.at[kind, p, c],
            device_id={"section": peer},
            device_id_type=MESH,
        )

    def share(kind, p, o):
        buf = h_all if kind == 0 else g_all
        return pltpu.make_async_remote_copy(
            src_ref=buf.at[p, d],
            dst_ref=buf.at[p, d],
            send_sem=all_send.at[kind, p, o - 1],
            recv_sem=all_recv.at[kind, p, o - 1],
            device_id={"dp": lax.rem(d + o, DP)},
            device_id_type=MESH,
        )

    def take(kind, p, o):
        buf = h_all if kind == 0 else g_all
        source = lax.rem(d + DP - o, DP)
        return pltpu.make_async_remote_copy(
            src_ref=buf.at[p, source],
            dst_ref=buf.at[p, source],
            send_sem=all_send.at[kind, p, o - 1],
            recv_sem=all_recv.at[kind, p, o - 1],
            device_id={"dp": source},
            device_id_type=MESH,
        )

    def share_start(kind, p):
        for o in range(1, DP):
            share(kind, p, o).start()

    def take_wait(kind, p):
        for o in range(1, DP):
            take(kind, p, o).wait_recv()

    def piece_of(i, b_ref, a_ref):
        if i < PIECES:
            return b_ref.at[:, pl.ds(i * (D // PIECES), D // PIECES)]
        return a_ref.at[:, pl.ds((i - PIECES) * (R // PIECES), R // PIECES)]

    def up_copy(i):
        return pltpu.make_async_remote_copy(
            src_ref=piece_of(i, up_b, up_a),
            dst_ref=piece_of(i, got_b, got_a),
            send_sem=up_send.at[i],
            recv_sem=up_recv.at[i],
            device_id={"section": mirror},
            device_id_type=MESH,
        )

    def via_copy(i):
        return pltpu.make_async_remote_copy(
            src_ref=piece_of(i, up_b, up_a),
            dst_ref=piece_of(i, via_b, via_a),
            send_sem=up_send.at[i],
            recv_sem=via_recv.at[i],
            device_id={"section": flip if i % 2 == 0 else cross},
            device_id_type=MESH,
        )

    def onward_copy(i):
        return pltpu.make_async_remote_copy(
            src_ref=piece_of(i, via_b, via_a),
            dst_ref=piece_of(i, got_b, got_a),
            send_sem=via_send.at[i],
            recv_sem=up_recv.at[i],
            device_id={"section": cross if i % 2 == 0 else flip},
            device_id_type=MESH,
        )

    def send_up(i):
        @pl.when(s >= S - S // 4)
        def _():
            via_copy(i).start()

        @pl.when(s < S - S // 4)
        def _():
            up_copy(i).start()

    def forward(p, k):
        load(0, win, wa, p).wait()

        @pl.when(k == 0)
        def _():
            feed_copy.wait()

        squares = jnp.zeros((M, 1), F32)
        for c in range(HOP_CHUNKS):
            part = pl.ds(c * cw, cw)

            @pl.when(k > 0)
            def _():
                hop(0, p, c).wait_recv()

            piece = h_all[p, d, :, part]
            wide = piece.astype(F32)
            squares += jnp.sum(wide * wide, axis=-1, keepdims=True)
            last = c == HOP_CHUNKS - 1
            if last:
                factor = lax.rsqrt(squares * (1.0 / D) + 1e-05)
            for u in range(UNIT_CHUNKS):
                cols = pl.ds(u * uw, uw)
                before = dot(piece, wa[p, part, cols])
                if c:
                    before += pre_own[p, :, cols]
                if last:
                    before *= factor
                    hid_own[:, cols] = (before * sigmoid(before)).astype(BF16)
                pre_own[p, :, cols] = before
        load(1, wout, wb, p).wait()
        for c in range(HOP_CHUNKS):
            cols = pl.ds(c * cw, cw)
            old = h_all[p, d, :, cols].astype(F32)
            h_out[p, :, cols] = (old + dot(hid_own[...], wb[p, :, cols])).astype(BF16)

            @pl.when(k < S - 1)
            def _():
                hop(0, p, c).start()

        share_start(0, p)
        u_own[p] = h_all[p, d].astype(F32) * factor
        r_own[p] = jnp.broadcast_to(factor, (M, 128))
        for u in range(UNIT_CHUNKS):
            cols = pl.ds(u * uw, uw)
            before = pre_own[p, :, cols]
            sigma = sigmoid(before)
            dsl_own[p, :, cols] = sigma * (1.0 + before * (1.0 - sigma))

    def backward(p, k):
        @pl.when(k == S - 1)
        def _():
            g_all[p, d] = (scale * h_out[p].astype(F32)).astype(BF16)

        @pl.when(k == 0)
        def _():
            for c in range(HOP_CHUNKS):
                hop(1, p, c).wait_recv()
            share_start(1, p)

        @pl.when(k > 0)
        def _():
            total = jnp.zeros((M, 1), F32)
            for c in range(HOP_CHUNKS):
                part = pl.ds(c * cw, cw)

                @pl.when(k < S - 1)
                def _():
                    hop(1, p, c).wait_recv()

                piece = g_all[p, d, :, part]
                for u in range(UNIT_CHUNKS):
                    cols = pl.ds(u * uw, uw)
                    d_hidden = dot_nt(piece, wb[p, cols, part])
                    if c:
                        d_hidden += dh_own[:, cols]
                    if c < HOP_CHUNKS - 1:
                        dh_own[:, cols] = d_hidden
                    else:
                        d_before = (d_hidden * dsl_own[p, :, cols]).astype(BF16)
                        dpre_own[:, cols] = d_before
                        total += jnp.sum(
                            d_before.astype(F32) * pre_own[p, :, cols], axis=-1, keepdims=True
                        )
            mean = total * (1.0 / D)
            factor = r_own[p, :, 0:1]
            for c in range(HOP_CHUNKS):
                cols = pl.ds(c * cw, cw)
                d_normed = dot_nt(dpre_own[...], wa[p, cols, :])
                out = g_all[p, d, :, cols].astype(F32) + factor * (
                    d_normed - u_own[p, :, cols] * mean
                )
                g_out[p, :, cols] = out.astype(BF16)
                hop(1, p, c).start()
            share_start(1, p)

    aligned = ra % 128 == 0 and rb % 128 == 0
    block = min(T, 256)

    def prepare(p):
        take_wait(0, p)

        def rows_step(b):
            per = block // M
            rows = pl.ds(pl.multiple_of(b * block, block), block)
            wide = h_all[p, pl.ds(b * per, per)].reshape(block, D).astype(F32)
            factor = norm_factor(wide)
            normed_wide = wide * factor
            normed = normed_wide.astype(BF16)
            if aligned:
                mine = h_all[
                    p, pl.ds(b * per, per), :, pl.ds(pl.multiple_of(d * ra, 128), ra)
                ].reshape(block, ra).astype(F32) * factor
                n_t[p, :, rows] = mine.T.astype(BF16)
                before = dot(normed, wa[p, :, pl.ds(pl.multiple_of(d * rb, 128), rb)])
                h_t[p, :, rows] = (before * sigmoid(before)).T.astype(BF16)
            else:
                full_t[0:D, rows] = normed_wide.T.astype(BF16)

            @pl.loop(0, UNIT_CHUNKS)
            def _(c):
                cols = unit_cols(c)
                before = dot(normed, wa[p, :, cols])
                sigma = sigmoid(before)
                dsl_all[p, rows, cols] = sigma * (1.0 + before * (1.0 - sigma))
                if not aligned:
                    full_t[pl.ds(pl.multiple_of(D + c * uw, 16), uw), rows] = (
                        (before * sigma).T.astype(BF16)
                    )

        if T == block:
            rows_step(0)
        else:
            pl.loop(0, T // block)(rows_step)
        if not aligned:
            n_t[p] = full_t[pl.ds(pl.multiple_of(d * ra, 16), ra), :]
            h_t[p] = full_t[pl.ds(pl.multiple_of(D + d * rb, 16), rb), :]

    def gradients(p):
        take_wait(1, p)
        term = dot(h_t[p], g_all[p].reshape(T, D))

        @pl.when(p == 1)
        def _():
            up_b[...] = term.astype(BF16)
            for i in range(PIECES):
                send_up(i)

        @pl.when(p == 0)
        def _():
            own_b[...] = term

        gw = R // GRAD_CHUNKS
        for c in range(GRAD_CHUNKS):
            cols = pl.ds(c * gw, gw)
            d_hidden = dot_nt(g_all[p].reshape(T, D), wb[p, cols, :])
            d_before = (d_hidden * dsl_all[p, :, cols]).astype(BF16)
            term = dot(n_t[p], d_before)

            @pl.when(p == 1)
            def _():
                up_a[:, cols] = term.astype(BF16)
                per = PIECES // GRAD_CHUNKS
                for i in range(per):
                    send_up(PIECES + c * per + i)

            @pl.when(p == 0)
            def _():
                own_a[:, cols] = term

    early = (k0 < S // 4).astype(jnp.int32)
    middle = (k0 == half - 1).astype(jnp.int32)

    @pl.loop(0, 4)
    def _(j):
        q = lax.rem((j + 1) // 2, 2)
        p = p0 + q * (1 - 2 * p0)
        k = k0 + q * (S - 1 - 2 * k0)

        @pl.when(j < 2)
        def _():
            forward(p, k)

        @pl.when(j >= 2)
        def _():
            backward(p, k)

        is1 = (j == 1).astype(jnp.int32)
        is2 = (j == 2).astype(jnp.int32)
        is3 = (j == 3).astype(jnp.int32)
        first = early * is2
        count = early * (1 - is1 - is3) + (1 - early) * 2 * is1

        @pl.loop(0, count)
        def _(i):
            prepare(p0 + (first + i) * (1 - 2 * p0))

        count = is2 * (1 - middle) + is3 * (1 + middle)

        @pl.loop(0, count)
        def _(i):
            which = is2 + is3 * (middle - i)
            gradients(p0 + which * (1 - 2 * p0))

    for lead, on_route in ((0, flip >= S - S // 4), (1, cross >= S - S // 4)):

        @pl.when(on_route)
        def _():
            for i in range(lead, 2 * PIECES, 2):
                via_copy(i).wait_recv()
                onward_copy(i).start()

    for i in range(2 * PIECES):
        up_copy(i).wait_recv()
        out, own, got = (ob, own_b, got_b) if i < PIECES else (oa, own_a, got_a)
        width = (D if i < PIECES else R) // PIECES
        cols = pl.ds((i % PIECES) * width, width)
        out[:, cols] = (own[:, cols] + got[:, cols].astype(F32)).astype(BF16)

    for c in range(HOP_CHUNKS):
        hop(0, p0, c).wait_send()
        hop(1, p1, c).wait_send()

    @pl.when(k0 > 0)
    def _():
        for c in range(HOP_CHUNKS):
            hop(0, p1, c).wait_send()
            hop(1, p0, c).wait_send()

    for kind in range(2):
        for p in (p0, p1):
            for o in range(1, DP):
                share(kind, p, o).wait_send()
    for i in range(2 * PIECES):
        up_copy(i).wait_send()
    for lead, on_route in ((0, flip >= S - S // 4), (1, cross >= S - S // 4)):

        @pl.when(on_route)
        def _():
            for i in range(lead, 2 * PIECES, 2):
                onward_copy(i).wait_send()


def widen_kernel(a_ref, b_ref, oa_ref, ob_ref):
    oa_ref[0] = a_ref[...].astype(F32)
    ob_ref[0] = b_ref[...].astype(F32)


def widen(a, b):
    parts = 2

    def narrow(x):
        return pl.BlockSpec((x.shape[0], x.shape[1] // parts), lambda i: (0, i))

    def wide(x):
        return pl.BlockSpec((1, x.shape[0], x.shape[1] // parts), lambda i: (0, 0, i))

    return pl.pallas_call(
        widen_kernel,
        grid=(parts,),
        out_shape=tuple(jax.ShapeDtypeStruct((1,) + x.shape, F32) for x in (a, b)),
        in_specs=[narrow(a), narrow(b)],
        out_specs=(wide(a), wide(b)),
        compiler_params=pltpu.CompilerParams(vmem_limit_bytes=60 * 1024 * 1024),
        cost_estimate=pl.CostEstimate(
            flops=a.size + b.size, bytes_accessed=6 * (a.size + b.size), transcendentals=0
        ),
    )(a, b)


def per_device(feed, proj_in, proj_out):
    S, DP = lax.axis_size("section"), lax.axis_size("dp")
    micro, rows, D = feed.shape[1:]
    R = proj_in.shape[3]
    M, T = micro * rows, micro * rows * DP
    ra, rb = D // DP, R // DP
    scale = 8.0 / T
    aligned = ra % 128 == 0 and rb % 128 == 0
    vm = pltpu.VMEM
    dma = pltpu.SemaphoreType.DMA
    peers = max(DP - 1, 1)
    grad_a, grad_b = pl.pallas_call(
        functools.partial(relay_kernel, S, DP, scale),
        out_shape=(
            jax.ShapeDtypeStruct((ra, R), BF16),
            jax.ShapeDtypeStruct((rb, D), BF16),
        ),
        in_specs=[pl.BlockSpec(memory_space=pltpu.HBM)] * 3,
        out_specs=(pl.BlockSpec(memory_space=pltpu.VMEM),) * 2,
        scratch_shapes=[
            vm((2, D, R), BF16),
            vm((2, R, D), BF16),
            vm((2, DP, M, D), BF16),
            vm((2, DP, M, D), BF16),
            vm((2, M, D), BF16),
            vm((2, M, D), BF16),
            vm((2, M, R), F32),
            vm((2, M, R), F32),
            vm((M, R), BF16),
            vm((M, R), BF16),
            vm((2, M, D), F32),
            vm((2, M, 128), F32),
            vm((2, ra, T), BF16),
            vm((2, rb, T), BF16),
            vm((2, T, R), F32),
            vm((ra, R), BF16),
            vm((rb, D), BF16),
            vm((ra, R), BF16),
            vm((rb, D), BF16),
            vm((ra, R), F32),
            vm((rb, D), F32),
            vm((M, R), F32),
            vm((ra, R), BF16),
            vm((rb, D), BF16),
            vm((16, 128) if aligned else (D + R, T), BF16),
            dma((2, 2)),
            dma(()),
            dma((2, 2, HOP_CHUNKS)),
            dma((2, 2, HOP_CHUNKS)),
            dma((2, 2, peers)),
            dma((2, 2, peers)),
            dma((2 * PIECES,)),
            dma((2 * PIECES,)),
            dma((2 * PIECES,)),
            dma((2 * PIECES,)),
        ],
        compiler_params=pltpu.CompilerParams(
            collective_id=0, has_side_effects=True, vmem_limit_bytes=60 * 1024 * 1024
        ),
        cost_estimate=pl.CostEstimate(
            flops=40 * M * D * R, bytes_accessed=16 * D * R, transcendentals=8 * T * R
        ),
    )(feed.reshape(2, M, D), proj_in, proj_out)
    return widen(grad_a, grad_b)


def solution(mesh):
    in_specs = (
        P(None, None, "dp", None),
        P(None, "section", None, None),
        P(None, "section", None, None),
    )
    out_specs = (P("section", "dp", None), P("section", "dp", None))
    return jax.shard_map(
        per_device, mesh=mesh, in_specs=in_specs, out_specs=out_specs, check_vma=False
    )
```

```python
import functools

import jax
import jax.numpy as jnp
from jax import lax
from jax.experimental import pallas as pl
from jax.experimental.pallas import tpu as pltpu
from jax.sharding import PartitionSpec as P

MESH = pl.DeviceIdType.MESH
F32, BF16 = jnp.float32, jnp.bfloat16
HOP_CHUNKS = 2
UNIT_CHUNKS = 3
GRAD_CHUNKS = 3


def dot(a, b):
    return jnp.dot(a, b, preferred_element_type=F32)


def dot_nt(a, b):
    return lax.dot_general(a, b, (((1,), (1,)), ((), ())), preferred_element_type=F32)


def sigmoid(x):
    return 0.5 + 0.5 * jnp.tanh(0.5 * x)


def norm_factor(wide):
    return lax.rsqrt(jnp.mean(wide * wide, axis=-1, keepdims=True) + 1e-05)


def relay_kernel(
    S, DP, scale,
    feed, win, wout, oa, ob,
    wa, wb, h_all, g_all, h_out, g_out, pre_own, dsl_own, hid_own, dpre_own, u_own, r_own,
    n_t, h_t, dsl_all, up_a, got_a, own_a, hm_t, dh_own, full_t,
    load_sem, feed_sem, hop_send, hop_recv, all_send, all_recv, up_send, up_recv, pair_send, pair_recv,
):
    s, d = lax.axis_index("section"), lax.axis_index("dp")
    M, D = h_all.shape[2], h_all.shape[3]
    R = wa.shape[2]
    T = DP * M
    ra, rb = D // DP, R // DP
    half = S // 2
    p0 = s // half
    p1 = 1 - p0
    k0 = s + p0 * (S - 1 - 2 * s)
    mirror = S - 1 - s
    cw, uw = D // HOP_CHUNKS, R // UNIT_CHUNKS

    def unit_cols(c):
        return pl.ds(pl.multiple_of(c * uw, uw), uw)

    def load(i, src, dst, p):
        return pltpu.make_async_copy(src.at[p, 0], dst.at[p], load_sem.at[i, p])

    feed_copy = pltpu.make_async_copy(feed.at[p0], h_all.at[p0, d], feed_sem)

    @pl.when(k0 == 0)
    def _():
        feed_copy.start()

    load(0, win, wa, p0).start()
    load(1, wout, wb, p0).start()

    barrier = pltpu.get_barrier_semaphore()
    for other in (lax.rem(s + 1, S), lax.rem(s + S - 1, S), mirror):
        pl.semaphore_signal(barrier, inc=1, device_id={"section": other}, device_id_type=MESH)
    for o in range(1, DP):
        pl.semaphore_signal(
            barrier, inc=1, device_id={"dp": lax.rem(d + o, DP)}, device_id_type=MESH
        )
    pl.semaphore_wait(barrier, 3 + DP - 1)

    load(0, win, wa, p1).start()
    load(1, wout, wb, p1).start()

    def hop(kind, p, c):
        step = 1 - 2 * p
        peer = s + step if kind == 0 else s - step
        src, dst = (h_out, h_all) if kind == 0 else (g_out, g_all)
        cols = pl.ds(c * cw, cw)
        return pltpu.make_async_remote_copy(
            src_ref=src.at[p, :, cols],
            dst_ref=dst.at[p, d, :, cols],
            send_sem=hop_send.at[kind, p, c],
            recv_sem=hop_recv.at[kind, p, c],
            device_id={"section": peer},
            device_id_type=MESH,
        )

    def share(kind, p, o):
        buf = h_all if kind == 0 else g_all
        return pltpu.make_async_remote_copy(
            src_ref=buf.at[p, d],
            dst_ref=buf.at[p, d],
            send_sem=all_send.at[kind, p, o - 1],
            recv_sem=all_recv.at[kind, p, o - 1],
            device_id={"dp": lax.rem(d + o, DP)},
            device_id_type=MESH,
        )

    def take(kind, p, o):
        buf = h_all if kind == 0 else g_all
        source = lax.rem(d + DP - o, DP)
        return pltpu.make_async_remote_copy(
            src_ref=buf.at[p, source],
            dst_ref=buf.at[p, source],
            send_sem=all_send.at[kind, p, o - 1],
            recv_sem=all_recv.at[kind, p, o - 1],
            device_id={"dp": source},
            device_id_type=MESH,
        )

    def share_start(kind, p):
        for o in range(1, DP):
            share(kind, p, o).start()

    def take_wait(kind, p):
        for o in range(1, DP):
            take(kind, p, o).wait_recv()

    gw = R // GRAD_CHUNKS

    def to_mirror(src, dst, send_sem, recv_sem):
        return pltpu.make_async_remote_copy(
            src_ref=src,
            dst_ref=dst,
            send_sem=send_sem,
            recv_sem=recv_sem,
            device_id={"section": mirror},
            device_id_type=MESH,
        )

    def up_copy(c):
        cols = pl.ds(c * gw, gw)
        return to_mirror(up_a.at[:, cols], got_a.at[:, cols], up_send.at[c], up_recv.at[c])

    def hidden_copy():
        return to_mirror(h_t.at[1], hm_t, pair_send.at[0], pair_recv.at[0])

    def seed_copy():
        return to_mirror(g_all.at[1, d], g_all.at[2, d], pair_send.at[1], pair_recv.at[1])

    def forward(p, k):
        load(0, win, wa, p).wait()

        @pl.when(k == 0)
        def _():
            feed_copy.wait()

        squares = jnp.zeros((M, 1), F32)
        for c in range(HOP_CHUNKS):
            part = pl.ds(c * cw, cw)

            @pl.when(k > 0)
            def _():
                hop(0, p, c).wait_recv()

            piece = h_all[p, d, :, part]
            wide = piece.astype(F32)
            squares += jnp.sum(wide * wide, axis=-1, keepdims=True)
            last = c == HOP_CHUNKS - 1
            if last:
                factor = lax.rsqrt(squares * (1.0 / D) + 1e-05)
            for u in range(UNIT_CHUNKS):
                cols = pl.ds(u * uw, uw)
                before = dot(piece, wa[p, part, cols])
                if c:
                    before += pre_own[p, :, cols]
                if last:
                    before *= factor
                    hid_own[:, cols] = (before * sigmoid(before)).astype(BF16)
                pre_own[p, :, cols] = before
        load(1, wout, wb, p).wait()
        for c in range(HOP_CHUNKS):
            cols = pl.ds(c * cw, cw)
            old = h_all[p, d, :, cols].astype(F32)
            h_out[p, :, cols] = (old + dot(hid_own[...], wb[p, :, cols])).astype(BF16)

            @pl.when(k < S - 1)
            def _():
                hop(0, p, c).start()

        share_start(0, p)
        u_own[p] = h_all[p, d].astype(F32) * factor
        r_own[p] = jnp.broadcast_to(factor, (M, 128))
        for u in range(UNIT_CHUNKS):
            cols = pl.ds(u * uw, uw)
            before = pre_own[p, :, cols]
            sigma = sigmoid(before)
            dsl_own[p, :, cols] = sigma * (1.0 + before * (1.0 - sigma))

    def seed_start(p):
        @pl.when(p == 1)
        def _():
            seed_copy().start()

    def backward(p, k):
        @pl.when(k == S - 1)
        def _():
            g_all[p, d] = (scale * h_out[p].astype(F32)).astype(BF16)

        @pl.when(k == 0)
        def _():
            for c in range(HOP_CHUNKS):
                hop(1, p, c).wait_recv()
            seed_start(p)
            share_start(1, p)

        @pl.when(k > 0)
        def _():
            total = jnp.zeros((M, 1), F32)
            for c in range(HOP_CHUNKS):
                part = pl.ds(c * cw, cw)

                @pl.when(k < S - 1)
                def _():
                    hop(1, p, c).wait_recv()

                piece = g_all[p, d, :, part]
                for u in range(UNIT_CHUNKS):
                    cols = pl.ds(u * uw, uw)
                    d_hidden = dot_nt(piece, wb[p, cols, part])
                    if c:
                        d_hidden += dh_own[:, cols]
                    if c < HOP_CHUNKS - 1:
                        dh_own[:, cols] = d_hidden
                    else:
                        d_before = (d_hidden * dsl_own[p, :, cols]).astype(BF16)
                        dpre_own[:, cols] = d_before
                        total += jnp.sum(
                            d_before.astype(F32) * pre_own[p, :, cols], axis=-1, keepdims=True
                        )
            mean = total * (1.0 / D)
            factor = r_own[p, :, 0:1]
            for c in range(HOP_CHUNKS):
                cols = pl.ds(c * cw, cw)
                d_normed = dot_nt(dpre_own[...], wa[p, cols, :])
                out = g_all[p, d, :, cols].astype(F32) + factor * (
                    d_normed - u_own[p, :, cols] * mean
                )
                g_out[p, :, cols] = out.astype(BF16)
                hop(1, p, c).start()
            seed_start(p)
            share_start(1, p)

    aligned = ra % 128 == 0 and rb % 128 == 0
    block = min(T, 256)

    def prepare(p):
        take_wait(0, p)

        def rows_step(b):
            per = block // M
            rows = pl.ds(pl.multiple_of(b * block, block), block)
            wide = h_all[p, pl.ds(b * per, per)].reshape(block, D).astype(F32)
            factor = norm_factor(wide)
            normed_wide = wide * factor
            normed = normed_wide.astype(BF16)
            if aligned:
                mine = h_all[
                    p, pl.ds(b * per, per), :, pl.ds(pl.multiple_of(d * ra, 128), ra)
                ].reshape(block, ra).astype(F32) * factor
                n_t[p, :, rows] = mine.T.astype(BF16)
                before = dot(normed, wa[p, :, pl.ds(pl.multiple_of(d * rb, 128), rb)])
                h_t[p, :, rows] = (before * sigmoid(before)).T.astype(BF16)
            else:
                full_t[0:D, rows] = normed_wide.T.astype(BF16)

            @pl.loop(0, UNIT_CHUNKS)
            def _(c):
                cols = unit_cols(c)
                before = dot(normed, wa[p, :, cols])
                sigma = sigmoid(before)
                dsl_all[p, rows, cols] = sigma * (1.0 + before * (1.0 - sigma))
                if not aligned:
                    full_t[pl.ds(pl.multiple_of(D + c * uw, 16), uw), rows] = (
                        (before * sigma).T.astype(BF16)
                    )

        if T == block:
            rows_step(0)
        else:
            pl.loop(0, T // block)(rows_step)
        if not aligned:
            n_t[p] = full_t[pl.ds(pl.multiple_of(d * ra, 16), ra), :]
            h_t[p] = full_t[pl.ds(pl.multiple_of(D + d * rb, 16), rb), :]

        @pl.when(p == 1)
        def _():
            hidden_copy().start()

    def gradients(p):
        take_wait(1, p)
        for c in range(GRAD_CHUNKS):
            cols = pl.ds(c * gw, gw)
            d_hidden = dot_nt(g_all[p].reshape(T, D), wb[p, cols, :])
            d_before = (d_hidden * dsl_all[p, :, cols]).astype(BF16)
            term = dot(n_t[p], d_before)

            @pl.when(p == 1)
            def _():
                up_a[:, cols] = term.astype(BF16)
                up_copy(c).start()

            @pl.when(p == 0)
            def _():
                own_a[:, cols] = term

        @pl.when(p == 0)
        def _():
            hidden_copy().wait_recv()
            take_wait(1, 2)
            ob[...] = (
                dot(h_t[0], g_all[0].reshape(T, D)) + dot(hm_t[...], g_all[2].reshape(T, D))
            ).astype(BF16)

    early = (k0 < S // 4).astype(jnp.int32)
    middle = (k0 == half - 1).astype(jnp.int32)

    @pl.loop(0, 4)
    def _(j):
        q = lax.rem((j + 1) // 2, 2)
        p = p0 + q * (1 - 2 * p0)
        k = k0 + q * (S - 1 - 2 * k0)

        @pl.when(j < 2)
        def _():
            forward(p, k)

        @pl.when(j >= 2)
        def _():
            backward(p, k)

        @pl.when((j >= 2) & (p == 0))
        def _():
            seed_copy().wait_recv()
            share_start(1, 2)

        is1 = (j == 1).astype(jnp.int32)
        is2 = (j == 2).astype(jnp.int32)
        is3 = (j == 3).astype(jnp.int32)
        first = early * is2
        count = early * (1 - is1 - is3) + (1 - early) * 2 * is1

        @pl.loop(0, count)
        def _(i):
            prepare(p0 + (first + i) * (1 - 2 * p0))

        count = is2 * (1 - middle) + is3 * (1 + middle)

        @pl.loop(0, count)
        def _(i):
            which = is2 + is3 * (middle - i)
            gradients(p0 + which * (1 - 2 * p0))

    for c in range(GRAD_CHUNKS):
        cols = pl.ds(c * gw, gw)
        up_copy(c).wait_recv()
        oa[:, cols] = (own_a[:, cols] + got_a[:, cols].astype(F32)).astype(BF16)

    for c in range(HOP_CHUNKS):
        hop(0, p0, c).wait_send()
        hop(1, p1, c).wait_send()

    @pl.when(k0 > 0)
    def _():
        for c in range(HOP_CHUNKS):
            hop(0, p1, c).wait_send()
            hop(1, p0, c).wait_send()

    for kind, p in ((0, 0), (0, 1), (1, 0), (1, 1), (1, 2)):
        for o in range(1, DP):
            share(kind, p, o).wait_send()
    hidden_copy().wait_send()
    seed_copy().wait_send()
    for c in range(GRAD_CHUNKS):
        up_copy(c).wait_send()


def widen_kernel(a_ref, b_ref, oa_ref, ob_ref):
    oa_ref[0] = a_ref[...].astype(F32)
    ob_ref[0] = b_ref[...].astype(F32)


def widen(a, b):
    parts = 2

    def narrow(x):
        return pl.BlockSpec((x.shape[0], x.shape[1] // parts), lambda i: (0, i))

    def wide(x):
        return pl.BlockSpec((1, x.shape[0], x.shape[1] // parts), lambda i: (0, 0, i))

    return pl.pallas_call(
        widen_kernel,
        grid=(parts,),
        out_shape=tuple(jax.ShapeDtypeStruct((1,) + x.shape, F32) for x in (a, b)),
        in_specs=[narrow(a), narrow(b)],
        out_specs=(wide(a), wide(b)),
        compiler_params=pltpu.CompilerParams(vmem_limit_bytes=60 * 1024 * 1024),
        cost_estimate=pl.CostEstimate(
            flops=a.size + b.size, bytes_accessed=6 * (a.size + b.size), transcendentals=0
        ),
    )(a, b)


def per_device(feed, proj_in, proj_out):
    S, DP = lax.axis_size("section"), lax.axis_size("dp")
    micro, rows, D = feed.shape[1:]
    R = proj_in.shape[3]
    M, T = micro * rows, micro * rows * DP
    ra, rb = D // DP, R // DP
    scale = 8.0 / T
    aligned = ra % 128 == 0 and rb % 128 == 0
    vm = pltpu.VMEM
    dma = pltpu.SemaphoreType.DMA
    peers = max(DP - 1, 1)
    grad_a, grad_b = pl.pallas_call(
        functools.partial(relay_kernel, S, DP, scale),
        out_shape=(
            jax.ShapeDtypeStruct((ra, R), BF16),
            jax.ShapeDtypeStruct((rb, D), BF16),
        ),
        in_specs=[pl.BlockSpec(memory_space=pltpu.HBM)] * 3,
        out_specs=(pl.BlockSpec(memory_space=pltpu.VMEM),) * 2,
        scratch_shapes=[
            vm((2, D, R), BF16),
            vm((2, R, D), BF16),
            vm((2, DP, M, D), BF16),
            vm((3, DP, M, D), BF16),
            vm((2, M, D), BF16),
            vm((2, M, D), BF16),
            vm((2, M, R), F32),
            vm((2, M, R), F32),
            vm((M, R), BF16),
            vm((M, R), BF16),
            vm((2, M, D), F32),
            vm((2, M, 128), F32),
            vm((2, ra, T), BF16),
            vm((2, rb, T), BF16),
            vm((2, T, R), F32),
            vm((ra, R), BF16),
            vm((ra, R), BF16),
            vm((ra, R), F32),
            vm((rb, T), BF16),
            vm((M, R), F32),
            vm((16, 128) if aligned else (D + R, T), BF16),
            dma((2, 2)),
            dma(()),
            dma((2, 2, HOP_CHUNKS)),
            dma((2, 2, HOP_CHUNKS)),
            dma((2, 3, peers)),
            dma((2, 3, peers)),
            dma((GRAD_CHUNKS,)),
            dma((GRAD_CHUNKS,)),
            dma((2,)),
            dma((2,)),
        ],
        compiler_params=pltpu.CompilerParams(
            collective_id=0, has_side_effects=True, vmem_limit_bytes=60 * 1024 * 1024
        ),
        cost_estimate=pl.CostEstimate(
            flops=40 * M * D * R, bytes_accessed=16 * D * R, transcendentals=8 * T * R
        ),
    )(feed.reshape(2, M, D), proj_in, proj_out)
    return widen(grad_a, grad_b)


def solution(mesh):
    in_specs = (
        P(None, None, "dp", None),
        P(None, "section", None, None),
        P(None, "section", None, None),
    )
    out_specs = (P("section", "dp", None), P("section", "dp", None))
    return jax.shard_map(
        per_device, mesh=mesh, in_specs=in_specs, out_specs=out_specs, check_vma=False
    )
```

```python
import functools

import jax
import jax.numpy as jnp
from jax import lax
from jax.experimental import pallas as pl
from jax.experimental.pallas import tpu as pltpu
from jax.sharding import PartitionSpec as P

MESH = pl.DeviceIdType.MESH
F32, BF16 = jnp.float32, jnp.bfloat16
HOP_CHUNKS = 2
UNIT_CHUNKS = 3
GRAD_CHUNKS = 3


def dot(a, b):
    return jnp.dot(a, b, preferred_element_type=F32)


def dot_nt(a, b):
    return lax.dot_general(a, b, (((1,), (1,)), ((), ())), preferred_element_type=F32)


def sigmoid(x):
    return 0.5 + 0.5 * jnp.tanh(0.5 * x)


def norm_factor(wide):
    return lax.rsqrt(jnp.mean(wide * wide, axis=-1, keepdims=True) + 1e-05)


def relay_kernel(
    S, DP, scale,
    feed, win, wout, oa, ob,
    wa, wb, h_all, g_all, h_out, g_out, pre_own, dsl_own, hid_own, dpre_own, u_own, r_own,
    n_t, h_t, dsl_all, up_a, got_a, own_a, own_b, hm_t, fin_a, fin_b, end_a, end_b,
    dh_own, full_t,
    load_sem, feed_sem, swap_send, swap_recv, hop_send, hop_recv, all_send, all_recv,
    up_send, up_recv, pair_send, pair_recv, fin_send, fin_recv,
):
    s, d = lax.axis_index("section"), lax.axis_index("dp")
    M, D = h_all.shape[2], h_all.shape[3]
    R = wa.shape[2]
    T = DP * M
    ra, rb = D // DP, R // DP
    last = S // 2 - 1
    p = lax.rem(s, 2)
    place = s // 2 + p * (last - 2 * (s // 2))
    mate = s + 1 - 2 * p
    stride = 2 * (1 - 2 * p)
    mirror = S - 1 - s
    cw, uw, gw = D // HOP_CHUNKS, R // UNIT_CHUNKS, R // GRAD_CHUNKS

    def unit_cols(c):
        return pl.ds(pl.multiple_of(c * uw, uw), uw)

    def load(i):
        src, dst = ((win, wa), (wout, wb))[i]
        return pltpu.make_async_copy(src.at[p, 0], dst.at[0], load_sem.at[i])

    def remote(src, dst, send_sem, recv_sem, section):
        return pltpu.make_async_remote_copy(
            src_ref=src,
            dst_ref=dst,
            send_sem=send_sem,
            recv_sem=recv_sem,
            device_id={"section": section},
            device_id_type=MESH,
        )

    def swap(i):
        src, dst = ((win, wa), (wout, wb))[i]
        return remote(src.at[1 - p, 0], dst.at[1], swap_send.at[i], swap_recv.at[i], mate)

    feed_copy = pltpu.make_async_copy(feed.at[p], h_all.at[0, d], feed_sem)

    @pl.when(place == 0)
    def _():
        feed_copy.start()

    load(0).start()
    load(1).start()

    barrier = pltpu.get_barrier_semaphore()
    for other in (mate, lax.rem(s + 2, S), lax.rem(s + S - 2, S), mirror):
        pl.semaphore_signal(barrier, inc=1, device_id={"section": other}, device_id_type=MESH)
    for o in range(1, DP):
        pl.semaphore_signal(
            barrier, inc=1, device_id={"dp": lax.rem(d + o, DP)}, device_id_type=MESH
        )
    pl.semaphore_wait(barrier, 4 + DP - 1)

    swap(0).start()
    swap(1).start()

    def hop(kind, c):
        cols = pl.ds(c * cw, cw)
        src, dst = ((h_out, h_all.at[0, d]), (g_out, g_all.at[1, d]))[kind]
        peer = s + stride if kind == 0 else s - stride
        return remote(
            src.at[:, cols], dst.at[:, cols], hop_send.at[kind, c], hop_recv.at[kind, c], peer
        )

    def share(kind, i, o, incoming=False):
        buf = (h_all, g_all)[kind]
        peer = lax.rem(d + (DP - o if incoming else o), DP)
        block = buf.at[i, peer if incoming else d]
        return pltpu.make_async_remote_copy(
            src_ref=block,
            dst_ref=block,
            send_sem=all_send.at[kind, i, o - 1],
            recv_sem=all_recv.at[kind, i, o - 1],
            device_id={"dp": peer},
            device_id_type=MESH,
        )

    def share_start(kind, i):
        for o in range(1, DP):
            share(kind, i, o).start()

    def take_wait(kind, i):
        for o in range(1, DP):
            share(kind, i, o, True).wait_recv()

    def up_copy(i, c):
        cols = pl.ds(c * gw, gw)
        return remote(
            up_a.at[i, :, cols], got_a.at[i, :, cols], up_send.at[i, c], up_recv.at[i, c], mirror
        )

    def hidden_copy(i):
        return remote(h_t.at[i], hm_t.at[i], pair_send.at[0, i], pair_recv.at[0, i], mirror)

    def seed_copy(i):
        return remote(
            g_all.at[i, d], g_all.at[2 + i, d], pair_send.at[1, i], pair_recv.at[1, i], mirror
        )

    def final_copy(i):
        src, dst = ((fin_a, end_a), (fin_b, end_b))[i]
        return remote(src, dst, fin_send.at[i], fin_recv.at[i], mate)

    def forward(i):
        steps = HOP_CHUNKS if i == 0 else 1
        width = D // steps
        squares = jnp.zeros((M, 1), F32)
        for c in range(steps):
            part = pl.ds(c * width, width)
            if i == 0:

                @pl.when(place > 0)
                def _():
                    hop(0, c).wait_recv()

            piece = h_all[i, d, :, part]
            wide = piece.astype(F32)
            squares += jnp.sum(wide * wide, axis=-1, keepdims=True)
            end = c == steps - 1
            if end:
                factor = lax.rsqrt(squares * (1.0 / D) + 1e-05)
            for u in range(UNIT_CHUNKS):
                cols = pl.ds(u * uw, uw)
                before = dot(piece, wa[i, part, cols])
                if c:
                    before += pre_own[i, :, cols]
                if end:
                    before *= factor
                    hid_own[:, cols] = (before * sigmoid(before)).astype(BF16)
                pre_own[i, :, cols] = before
        if i == 0:
            load(1).wait()
        else:
            swap(1).wait_recv()
        for c in range(HOP_CHUNKS):
            cols = pl.ds(c * cw, cw)
            old = h_all[i, d, :, cols].astype(F32)
            new = (old + dot(hid_own[...], wb[i, :, cols])).astype(BF16)
            if i == 0:
                h_all[1, d, :, cols] = new
            else:
                h_out[:, cols] = new

                @pl.when(place < last)
                def _():
                    hop(0, c).start()

    def forward_rest(i):
        share_start(0, i)
        wide = h_all[i, d].astype(F32)
        factor = norm_factor(wide)
        u_own[i] = wide * factor
        r_own[i] = jnp.broadcast_to(factor, (M, 128))
        for u in range(UNIT_CHUNKS):
            cols = pl.ds(u * uw, uw)
            before = pre_own[i, :, cols]
            sigma = sigmoid(before)
            dsl_own[i, :, cols] = sigma * (1.0 + before * (1.0 - sigma))

    def spread(i):
        share_start(1, i)

        @pl.when(p == 1)
        def _():
            seed_copy(i).start()

    def backward(i):
        steps = HOP_CHUNKS if i == 1 else 1
        width = D // steps
        total = jnp.zeros((M, 1), F32)
        for c in range(steps):
            part = pl.ds(c * width, width)
            if i == 1:

                @pl.when(place < last)
                def _():
                    hop(1, c).wait_recv()

                if c == steps - 1:
                    spread(1)

            piece = g_all[i, d, :, part]
            for u in range(UNIT_CHUNKS):
                cols = pl.ds(u * uw, uw)
                d_hidden = dot_nt(piece, wb[i, cols, part])
                if c:
                    d_hidden += dh_own[:, cols]
                if c < steps - 1:
                    dh_own[:, cols] = d_hidden
                else:
                    d_before = (d_hidden * dsl_own[i, :, cols]).astype(BF16)
                    dpre_own[:, cols] = d_before
                    total += jnp.sum(
                        d_before.astype(F32) * pre_own[i, :, cols], axis=-1, keepdims=True
                    )
        mean = total * (1.0 / D)
        factor = r_own[i, :, 0:1]
        for c in range(HOP_CHUNKS):
            cols = pl.ds(c * cw, cw)
            d_normed = dot_nt(dpre_own[...], wa[i, cols, :])
            out = g_all[i, d, :, cols].astype(F32) + factor * (
                d_normed - u_own[i, :, cols] * mean
            )
            if i == 1:
                g_all[0, d, :, cols] = out.astype(BF16)
            else:
                g_out[:, cols] = out.astype(BF16)
                hop(1, c).start()

    aligned = ra % 128 == 0 and rb % 128 == 0
    block = min(T, 256)

    def prepare(i):
        take_wait(0, i)

        def rows_step(b):
            per = block // M
            rows = pl.ds(pl.multiple_of(b * block, block), block)
            wide = h_all[i, pl.ds(b * per, per)].reshape(block, D).astype(F32)
            factor = norm_factor(wide)
            normed_wide = wide * factor
            normed = normed_wide.astype(BF16)
            if aligned:
                mine = h_all[
                    i, pl.ds(b * per, per), :, pl.ds(pl.multiple_of(d * ra, 128), ra)
                ].reshape(block, ra).astype(F32) * factor
                n_t[i, :, rows] = mine.T.astype(BF16)
                before = dot(normed, wa[i, :, pl.ds(pl.multiple_of(d * rb, 128), rb)])
                h_t[i, :, rows] = (before * sigmoid(before)).T.astype(BF16)
            else:
                full_t[0:D, rows] = normed_wide.T.astype(BF16)

            @pl.loop(0, UNIT_CHUNKS)
            def _(c):
                cols = unit_cols(c)
                before = dot(normed, wa[i, :, cols])
                sigma = sigmoid(before)
                dsl_all[i, rows, cols] = sigma * (1.0 + before * (1.0 - sigma))
                if not aligned:
                    full_t[pl.ds(pl.multiple_of(D + c * uw, 16), uw), rows] = (
                        (before * sigma).T.astype(BF16)
                    )

        if T == block:
            rows_step(0)
        else:
            pl.loop(0, T // block)(rows_step)
        if not aligned:
            n_t[i] = full_t[pl.ds(pl.multiple_of(d * ra, 16), ra), :]
            h_t[i] = full_t[pl.ds(pl.multiple_of(D + d * rb, 16), rb), :]

        @pl.when(p == 1)
        def _():
            hidden_copy(i).start()

    def gradients(i):
        take_wait(1, i)
        for c in range(GRAD_CHUNKS):
            cols = pl.ds(c * gw, gw)
            d_hidden = dot_nt(g_all[i].reshape(T, D), wb[i, cols, :])
            d_before = (d_hidden * dsl_all[i, :, cols]).astype(BF16)
            term = dot(n_t[i], d_before)

            @pl.when(p == 1)
            def _():
                up_a[i, :, cols] = term.astype(BF16)
                up_copy(i, c).start()

            @pl.when(p == 0)
            def _():
                own_a[i, :, cols] = term

        @pl.when(p == 0)
        def _():
            own_b[i] = dot(h_t[i], g_all[i].reshape(T, D))

    def finish(i, out_a, out_b):
        hidden_copy(i).wait_recv()
        take_wait(1, 2 + i)
        out_b[...] = (own_b[i] + dot(hm_t[i], g_all[2 + i].reshape(T, D))).astype(BF16)
        for c in range(GRAD_CHUNKS):
            cols = pl.ds(c * gw, gw)
            up_copy(i, c).wait_recv()
            out_a[:, cols] = (own_a[i, :, cols] + got_a[i, :, cols].astype(F32)).astype(BF16)

    load(0).wait()

    @pl.when(place == 0)
    def _():
        feed_copy.wait()

    forward(0)
    swap(0).wait_recv()
    forward(1)

    @pl.when(place == last)
    def _():
        g_all[1, d] = (scale * h_out[...].astype(F32)).astype(BF16)

    for i in range(2):
        forward_rest(i)

    @pl.when(place < last)
    def _():
        pl.loop(0, 2)(prepare)

    backward(1)

    @pl.when(p == 0)
    def _():
        seed_copy(1).wait_recv()
        share_start(1, 3)

    @pl.when(place > 0)
    def _():
        backward(0)

    spread(0)

    @pl.when(p == 0)
    def _():
        seed_copy(0).wait_recv()
        share_start(1, 2)

    @pl.when(place == last)
    def _():
        pl.loop(0, 2)(prepare)

    gradients(1)
    gradients(0)

    @pl.when(p == 0)
    def _():
        finish(1, fin_a, fin_b)
        final_copy(0).start()
        final_copy(1).start()
        finish(0, oa, ob)

    @pl.when(p == 1)
    def _():
        final_copy(0).wait_recv()
        oa[...] = end_a[...]
        final_copy(1).wait_recv()
        ob[...] = end_b[...]

    for i in range(2):
        swap(i).wait_send()

    for kind, sent in ((0, place < last), (1, place > 0)):

        @pl.when(sent)
        def _():
            for c in range(HOP_CHUNKS):
                hop(kind, c).wait_send()

        for i in range(2):
            for o in range(1, DP):
                share(kind, i, o).wait_send()

    @pl.when(p == 0)
    def _():
        for i in range(2):
            final_copy(i).wait_send()
            for o in range(1, DP):
                share(1, 2 + i, o).wait_send()

    @pl.when(p == 1)
    def _():
        for i in range(2):
            hidden_copy(i).wait_send()
            seed_copy(i).wait_send()
            for c in range(GRAD_CHUNKS):
                up_copy(i, c).wait_send()


def widen_kernel(a_ref, b_ref, oa_ref, ob_ref):
    oa_ref[0] = a_ref[...].astype(F32)
    ob_ref[0] = b_ref[...].astype(F32)


def widen(a, b):
    parts = 2

    def narrow(x):
        return pl.BlockSpec((x.shape[0], x.shape[1] // parts), lambda i: (0, i))

    def wide(x):
        return pl.BlockSpec((1, x.shape[0], x.shape[1] // parts), lambda i: (0, 0, i))

    return pl.pallas_call(
        widen_kernel,
        grid=(parts,),
        out_shape=tuple(jax.ShapeDtypeStruct((1,) + x.shape, F32) for x in (a, b)),
        in_specs=[narrow(a), narrow(b)],
        out_specs=(wide(a), wide(b)),
        compiler_params=pltpu.CompilerParams(vmem_limit_bytes=60 * 1024 * 1024),
        cost_estimate=pl.CostEstimate(
            flops=a.size + b.size, bytes_accessed=6 * (a.size + b.size), transcendentals=0
        ),
    )(a, b)


def per_device(feed, proj_in, proj_out):
    S, DP = lax.axis_size("section"), lax.axis_size("dp")
    micro, rows, D = feed.shape[1:]
    R = proj_in.shape[3]
    M, T = micro * rows, micro * rows * DP
    ra, rb = D // DP, R // DP
    scale = 8.0 / T
    aligned = ra % 128 == 0 and rb % 128 == 0
    vm = pltpu.VMEM
    dma = pltpu.SemaphoreType.DMA
    peers = max(DP - 1, 1)
    grad_a, grad_b = pl.pallas_call(
        functools.partial(relay_kernel, S, DP, scale),
        out_shape=(
            jax.ShapeDtypeStruct((ra, R), BF16),
            jax.ShapeDtypeStruct((rb, D), BF16),
        ),
        in_specs=[pl.BlockSpec(memory_space=pltpu.HBM)] * 3,
        out_specs=(pl.BlockSpec(memory_space=pltpu.VMEM),) * 2,
        scratch_shapes=[
            vm((2, D, R), BF16),
            vm((2, R, D), BF16),
            vm((2, DP, M, D), BF16),
            vm((4, DP, M, D), BF16),
            vm((M, D), BF16),
            vm((M, D), BF16),
            vm((2, M, R), F32),
            vm((2, M, R), F32),
            vm((M, R), BF16),
            vm((M, R), BF16),
            vm((2, M, D), F32),
            vm((2, M, 128), F32),
            vm((2, ra, T), BF16),
            vm((2, rb, T), BF16),
            vm((2, T, R), F32),
            vm((2, ra, R), BF16),
            vm((2, ra, R), BF16),
            vm((2, ra, R), F32),
            vm((2, rb, D), F32),
            vm((2, rb, T), BF16),
            vm((ra, R), BF16),
            vm((rb, D), BF16),
            vm((ra, R), BF16),
            vm((rb, D), BF16),
            vm((M, R), F32),
            vm((16, 128) if aligned else (D + R, T), BF16),
            dma((2,)),
            dma(()),
            dma((2,)),
            dma((2,)),
            dma((2, HOP_CHUNKS)),
            dma((2, HOP_CHUNKS)),
            dma((2, 4, peers)),
            dma((2, 4, peers)),
            dma((2, GRAD_CHUNKS)),
            dma((2, GRAD_CHUNKS)),
            dma((2, 2)),
            dma((2, 2)),
            dma((2,)),
            dma((2,)),
        ],
        compiler_params=pltpu.CompilerParams(
            collective_id=0, has_side_effects=True, vmem_limit_bytes=60 * 1024 * 1024
        ),
        cost_estimate=pl.CostEstimate(
            flops=40 * M * D * R, bytes_accessed=16 * D * R, transcendentals=8 * T * R
        ),
    )(feed.reshape(2, M, D), proj_in, proj_out)
    return widen(grad_a, grad_b)


def solution(mesh):
    in_specs = (
        P(None, None, "dp", None),
        P(None, "section", None, None),
        P(None, "section", None, None),
    )
    out_specs = (P("section", "dp", None), P("section", "dp", None))
    return jax.shard_map(
        per_device, mesh=mesh, in_specs=in_specs, out_specs=out_specs, check_vma=False
    )
```

```python
import functools

import jax
import jax.numpy as jnp
from jax import lax
from jax.experimental import pallas as pl
from jax.experimental.pallas import tpu as pltpu
from jax.sharding import PartitionSpec as P

MESH = pl.DeviceIdType.MESH
F32, BF16 = jnp.float32, jnp.bfloat16
HOP_CHUNKS = 2
UNIT_CHUNKS = 3
GRAD_CHUNKS = 3


def dot(a, b):
    return jnp.dot(a, b, preferred_element_type=F32)


def sigmoid(x):
    return 0.5 + 0.5 * jnp.tanh(0.5 * x)


def norm_factor(wide):
    return lax.rsqrt(jnp.mean(wide * wide, axis=-1, keepdims=True) + 1e-05)


def relay_kernel(
    S, DP, scale,
    feed, win, wout, oa, ob,
    wa, wb, wat, wbt, h_all, g_all, h_out, g_out, pre_own, dsl_own, hid_own, dpre_own, u_own, r_own,
    n_t, h_t, dsl_all, up_a, got_a, own_a, own_b, hm_t, fin_a, fin_b, end_a, end_b,
    dh_own, full_t,
    load_sem, feed_sem, swap_send, swap_recv, hop_send, hop_recv, all_send, all_recv,
    up_send, up_recv, pair_send, pair_recv, fin_send, fin_recv,
):
    s, d = lax.axis_index("section"), lax.axis_index("dp")
    M, D = h_all.shape[2], h_all.shape[3]
    R = wa.shape[2]
    T = DP * M
    ra, rb = D // DP, R // DP
    last = S // 2 - 1
    p = lax.rem(s, 2)
    place = s // 2 + p * (last - 2 * (s // 2))
    mate = s + 1 - 2 * p
    stride = 2 * (1 - 2 * p)
    mirror = S - 1 - s
    cw, uw, gw = D // HOP_CHUNKS, R // UNIT_CHUNKS, R // GRAD_CHUNKS

    def unit_cols(c):
        return pl.ds(pl.multiple_of(c * uw, uw), uw)

    def load(i):
        src, dst = ((win, wa), (wout, wb))[i]
        return pltpu.make_async_copy(src.at[p, 0], dst.at[0], load_sem.at[i])

    def remote(src, dst, send_sem, recv_sem, section):
        return pltpu.make_async_remote_copy(
            src_ref=src,
            dst_ref=dst,
            send_sem=send_sem,
            recv_sem=recv_sem,
            device_id={"section": section},
            device_id_type=MESH,
        )

    def swap(i):
        src, dst = ((win, wa), (wout, wb))[i]
        return remote(src.at[1 - p, 0], dst.at[1], swap_send.at[i], swap_recv.at[i], mate)

    feed_copy = pltpu.make_async_copy(feed.at[p], h_all.at[0, d], feed_sem)

    @pl.when(place == 0)
    def _():
        feed_copy.start()

    load(0).start()
    load(1).start()

    barrier = pltpu.get_barrier_semaphore()
    for other in (mate, lax.rem(s + 2, S), lax.rem(s + S - 2, S), mirror):
        pl.semaphore_signal(barrier, inc=1, device_id={"section": other}, device_id_type=MESH)
    for o in range(1, DP):
        pl.semaphore_signal(
            barrier, inc=1, device_id={"dp": lax.rem(d + o, DP)}, device_id_type=MESH
        )
    pl.semaphore_wait(barrier, 4 + DP - 1)

    swap(0).start()
    swap(1).start()

    def hop(kind, c):
        cols = pl.ds(c * cw, cw)
        src, dst = ((h_out, h_all.at[0, d]), (g_out, g_all.at[1, d]))[kind]
        peer = s + stride if kind == 0 else s - stride
        return remote(
            src.at[:, cols], dst.at[:, cols], hop_send.at[kind, c], hop_recv.at[kind, c], peer
        )

    def share(kind, i, o, incoming=False):
        buf = (h_all, g_all)[kind]
        peer = lax.rem(d + (DP - o if incoming else o), DP)
        block = buf.at[i, peer if incoming else d]
        return pltpu.make_async_remote_copy(
            src_ref=block,
            dst_ref=block,
            send_sem=all_send.at[kind, i, o - 1],
            recv_sem=all_recv.at[kind, i, o - 1],
            device_id={"dp": peer},
            device_id_type=MESH,
        )

    def share_start(kind, i):
        for o in range(1, DP):
            share(kind, i, o).start()

    def take_wait(kind, i):
        for o in range(1, DP):
            share(kind, i, o, True).wait_recv()

    def up_copy(i, c):
        cols = pl.ds(c * gw, gw)
        return remote(
            up_a.at[i, :, cols], got_a.at[i, :, cols], up_send.at[i, c], up_recv.at[i, c], mirror
        )

    def hidden_copy(i):
        return remote(h_t.at[i], hm_t.at[i], pair_send.at[0, i], pair_recv.at[0, i], mirror)

    def seed_copy(i):
        return remote(
            g_all.at[i, d], g_all.at[2 + i, d], pair_send.at[1, i], pair_recv.at[1, i], mirror
        )

    def final_copy(i):
        src, dst = ((fin_a, end_a), (fin_b, end_b))[i]
        return remote(src, dst, fin_send.at[i], fin_recv.at[i], mate)

    def forward(i):
        steps = HOP_CHUNKS if i == 0 else 1
        width = D // steps
        squares = jnp.zeros((M, 1), F32)
        for c in range(steps):
            part = pl.ds(c * width, width)
            if i == 0:

                @pl.when(place > 0)
                def _():
                    hop(0, c).wait_recv()

            piece = h_all[i, d, :, part]
            wide = piece.astype(F32)
            squares += jnp.sum(wide * wide, axis=-1, keepdims=True)
            end = c == steps - 1
            if end:
                factor = lax.rsqrt(squares * (1.0 / D) + 1e-05)
            for u in range(UNIT_CHUNKS):
                cols = pl.ds(u * uw, uw)
                before = dot(piece, wa[i, part, cols])
                if c:
                    before += pre_own[i, :, cols]
                if end:
                    before *= factor
                    hid_own[:, cols] = (before * sigmoid(before)).astype(BF16)
                pre_own[i, :, cols] = before

        @pl.when(place < last)
        def _():
            if i == 0:
                load(1).wait()
            else:
                swap(1).wait_recv()

        for c in range(HOP_CHUNKS):
            cols = pl.ds(c * cw, cw)
            old = h_all[i, d, :, cols].astype(F32)
            new = (old + dot(hid_own[...], wb[i, :, cols])).astype(BF16)
            if i == 0:
                h_all[1, d, :, cols] = new
            else:
                h_out[:, cols] = new

                @pl.when(place < last)
                def _():
                    hop(0, c).start()

    def forward_rest(i):
        share_start(0, i)
        wide = h_all[i, d].astype(F32)
        factor = norm_factor(wide)
        u_own[i] = wide * factor
        r_own[i] = jnp.broadcast_to(factor, (M, 128))
        for u in range(UNIT_CHUNKS):
            cols = pl.ds(u * uw, uw)
            before = pre_own[i, :, cols]
            sigma = sigmoid(before)
            dsl_own[i, :, cols] = sigma * (1.0 + before * (1.0 - sigma))

    def spread(i):
        share_start(1, i)

        @pl.when(p == 1)
        def _():
            seed_copy(i).start()

    def backward(i):
        steps = HOP_CHUNKS if i == 1 else 1
        width = D // steps
        total = jnp.zeros((M, 1), F32)
        for c in range(steps):
            part = pl.ds(c * width, width)
            if i == 1:

                @pl.when(place < last)
                def _():
                    hop(1, c).wait_recv()

                if c == steps - 1:
                    spread(1)

            piece = g_all[i, d, :, part]
            for u in range(UNIT_CHUNKS):
                cols = pl.ds(u * uw, uw)
                d_hidden = dot(piece, wbt[i, part, cols])
                if c:
                    d_hidden += dh_own[:, cols]
                if c < steps - 1:
                    dh_own[:, cols] = d_hidden
                else:
                    d_before = (d_hidden * dsl_own[i, :, cols]).astype(BF16)
                    dpre_own[:, cols] = d_before
                    total += jnp.sum(
                        d_before.astype(F32) * pre_own[i, :, cols], axis=-1, keepdims=True
                    )
        mean = total * (1.0 / D)
        factor = r_own[i, :, 0:1]
        for c in range(HOP_CHUNKS):
            cols = pl.ds(c * cw, cw)
            d_normed = dot(dpre_own[...], wat[i, :, cols])
            out = g_all[i, d, :, cols].astype(F32) + factor * (
                d_normed - u_own[i, :, cols] * mean
            )
            if i == 1:
                g_all[0, d, :, cols] = out.astype(BF16)
            else:
                g_out[:, cols] = out.astype(BF16)
                hop(1, c).start()

    aligned = ra % 128 == 0 and rb % 128 == 0
    block = min(T, 256)

    def prepare(i):
        take_wait(0, i)

        def rows_step(b):
            per = block // M
            rows = pl.ds(pl.multiple_of(b * block, block), block)
            wide = h_all[i, pl.ds(b * per, per)].reshape(block, D).astype(F32)
            factor = norm_factor(wide)
            normed_wide = wide * factor
            normed = normed_wide.astype(BF16)
            if aligned:
                mine = h_all[
                    i, pl.ds(b * per, per), :, pl.ds(pl.multiple_of(d * ra, 128), ra)
                ].reshape(block, ra).astype(F32) * factor
                n_t[i, :, rows] = mine.T.astype(BF16)
                before = dot(normed, wa[i, :, pl.ds(pl.multiple_of(d * rb, 128), rb)])
                h_t[i, :, rows] = (before * sigmoid(before)).T.astype(BF16)
            else:
                full_t[0:D, rows] = normed_wide.T.astype(BF16)

            @pl.loop(0, UNIT_CHUNKS)
            def _(c):
                cols = unit_cols(c)
                before = dot(normed, wa[i, :, cols])
                sigma = sigmoid(before)
                dsl_all[i, rows, cols] = sigma * (1.0 + before * (1.0 - sigma))
                if not aligned:
                    full_t[pl.ds(pl.multiple_of(D + c * uw, 16), uw), rows] = (
                        (before * sigma).T.astype(BF16)
                    )

        if T == block:
            rows_step(0)
        else:
            pl.loop(0, T // block)(rows_step)
        if not aligned:
            n_t[i] = full_t[pl.ds(pl.multiple_of(d * ra, 16), ra), :]
            h_t[i] = full_t[pl.ds(pl.multiple_of(D + d * rb, 16), rb), :]

        @pl.when(p == 1)
        def _():
            hidden_copy(i).start()

    def gradients(i):
        take_wait(1, i)
        for c in range(GRAD_CHUNKS):
            cols = pl.ds(c * gw, gw)
            d_hidden = dot(g_all[i].reshape(T, D), wbt[i, :, cols])
            d_before = (d_hidden * dsl_all[i, :, cols]).astype(BF16)
            term = dot(n_t[i], d_before)

            @pl.when(p == 1)
            def _():
                up_a[i, :, cols] = term.astype(BF16)
                up_copy(i, c).start()

            @pl.when(p == 0)
            def _():
                own_a[i, :, cols] = term

        @pl.when(p == 0)
        def _():
            own_b[i] = dot(h_t[i], g_all[i].reshape(T, D))

    def finish(i, out_a, out_b):
        hidden_copy(i).wait_recv()
        take_wait(1, 2 + i)
        out_b[...] = (own_b[i] + dot(hm_t[i], g_all[2 + i].reshape(T, D))).astype(BF16)
        for c in range(GRAD_CHUNKS):
            cols = pl.ds(c * gw, gw)
            up_copy(i, c).wait_recv()
            out_a[:, cols] = (own_a[i, :, cols] + got_a[i, :, cols].astype(F32)).astype(BF16)

    def turn_weights():
        @pl.loop(0, 2)
        def _(i):
            @pl.loop(0, UNIT_CHUNKS)
            def _(c):
                cols = unit_cols(c)
                wbt[i, :, cols] = wb[i, cols, :].T
                wat[i, cols, :] = wa[i, :, cols].T

    load(0).wait()

    @pl.when(place == last)
    def _():
        load(1).wait()
        for i in range(2):
            swap(i).wait_recv()
        turn_weights()

    @pl.when(place == 0)
    def _():
        feed_copy.wait()

    forward(0)

    @pl.when(place < last)
    def _():
        swap(0).wait_recv()

    forward(1)

    @pl.when(place == last)
    def _():
        g_all[1, d] = (scale * h_out[...].astype(F32)).astype(BF16)

    for i in range(2):
        forward_rest(i)

    @pl.when(place < last)
    def _():
        turn_weights()
        pl.loop(0, 2)(prepare)

    backward(1)

    @pl.when(p == 0)
    def _():
        seed_copy(1).wait_recv()
        share_start(1, 3)

    @pl.when(place > 0)
    def _():
        backward(0)

    spread(0)

    @pl.when(p == 0)
    def _():
        seed_copy(0).wait_recv()
        share_start(1, 2)

    @pl.when(place == last)
    def _():
        pl.loop(0, 2)(prepare)

    gradients(1)
    gradients(0)

    @pl.when(p == 0)
    def _():
        finish(1, fin_a, fin_b)
        final_copy(0).start()
        final_copy(1).start()
        finish(0, oa, ob)

    @pl.when(p == 1)
    def _():
        final_copy(0).wait_recv()
        oa[...] = end_a[...]
        final_copy(1).wait_recv()
        ob[...] = end_b[...]

    for i in range(2):
        swap(i).wait_send()

    for kind, sent in ((0, place < last), (1, place > 0)):

        @pl.when(sent)
        def _():
            for c in range(HOP_CHUNKS):
                hop(kind, c).wait_send()

        for i in range(2):
            for o in range(1, DP):
                share(kind, i, o).wait_send()

    @pl.when(p == 0)
    def _():
        for i in range(2):
            final_copy(i).wait_send()
            for o in range(1, DP):
                share(1, 2 + i, o).wait_send()

    @pl.when(p == 1)
    def _():
        for i in range(2):
            hidden_copy(i).wait_send()
            seed_copy(i).wait_send()
            for c in range(GRAD_CHUNKS):
                up_copy(i, c).wait_send()


def widen_kernel(a_ref, b_ref, oa_ref, ob_ref):
    oa_ref[0] = a_ref[...].astype(F32)
    ob_ref[0] = b_ref[...].astype(F32)


def widen(a, b):
    parts = 2

    def narrow(x):
        return pl.BlockSpec((x.shape[0], x.shape[1] // parts), lambda i: (0, i))

    def wide(x):
        return pl.BlockSpec((1, x.shape[0], x.shape[1] // parts), lambda i: (0, 0, i))

    return pl.pallas_call(
        widen_kernel,
        grid=(parts,),
        out_shape=tuple(jax.ShapeDtypeStruct((1,) + x.shape, F32) for x in (a, b)),
        in_specs=[narrow(a), narrow(b)],
        out_specs=(wide(a), wide(b)),
        compiler_params=pltpu.CompilerParams(vmem_limit_bytes=60 * 1024 * 1024),
        cost_estimate=pl.CostEstimate(
            flops=a.size + b.size, bytes_accessed=6 * (a.size + b.size), transcendentals=0
        ),
    )(a, b)


def per_device(feed, proj_in, proj_out):
    S, DP = lax.axis_size("section"), lax.axis_size("dp")
    micro, rows, D = feed.shape[1:]
    R = proj_in.shape[3]
    M, T = micro * rows, micro * rows * DP
    ra, rb = D // DP, R // DP
    scale = 8.0 / T
    aligned = ra % 128 == 0 and rb % 128 == 0
    vm = pltpu.VMEM
    dma = pltpu.SemaphoreType.DMA
    peers = max(DP - 1, 1)
    grad_a, grad_b = pl.pallas_call(
        functools.partial(relay_kernel, S, DP, scale),
        out_shape=(
            jax.ShapeDtypeStruct((ra, R), BF16),
            jax.ShapeDtypeStruct((rb, D), BF16),
        ),
        in_specs=[pl.BlockSpec(memory_space=pltpu.HBM)] * 3,
        out_specs=(pl.BlockSpec(memory_space=pltpu.VMEM),) * 2,
        scratch_shapes=[
            vm((2, D, R), BF16),
            vm((2, R, D), BF16),
            vm((2, R, D), BF16),
            vm((2, D, R), BF16),
            vm((2, DP, M, D), BF16),
            vm((4, DP, M, D), BF16),
            vm((M, D), BF16),
            vm((M, D), BF16),
            vm((2, M, R), F32),
            vm((2, M, R), F32),
            vm((M, R), BF16),
            vm((M, R), BF16),
            vm((2, M, D), F32),
            vm((2, M, 128), F32),
            vm((2, ra, T), BF16),
            vm((2, rb, T), BF16),
            vm((2, T, R), F32),
            vm((2, ra, R), BF16),
            vm((2, ra, R), BF16),
            vm((2, ra, R), F32),
            vm((2, rb, D), F32),
            vm((2, rb, T), BF16),
            vm((ra, R), BF16),
            vm((rb, D), BF16),
            vm((ra, R), BF16),
            vm((rb, D), BF16),
            vm((M, R), F32),
            vm((16, 128) if aligned else (D + R, T), BF16),
            dma((2,)),
            dma(()),
            dma((2,)),
            dma((2,)),
            dma((2, HOP_CHUNKS)),
            dma((2, HOP_CHUNKS)),
            dma((2, 4, peers)),
            dma((2, 4, peers)),
            dma((2, GRAD_CHUNKS)),
            dma((2, GRAD_CHUNKS)),
            dma((2, 2)),
            dma((2, 2)),
            dma((2,)),
            dma((2,)),
        ],
        compiler_params=pltpu.CompilerParams(
            collective_id=0, has_side_effects=True, vmem_limit_bytes=60 * 1024 * 1024
        ),
        cost_estimate=pl.CostEstimate(
            flops=40 * M * D * R, bytes_accessed=16 * D * R, transcendentals=8 * T * R
        ),
    )(feed.reshape(2, M, D), proj_in, proj_out)
    return widen(grad_a, grad_b)


def solution(mesh):
    in_specs = (
        P(None, None, "dp", None),
        P(None, "section", None, None),
        P(None, "section", None, None),
    )
    out_specs = (P("section", "dp", None), P("section", "dp", None))
    return jax.shard_map(
        per_device, mesh=mesh, in_specs=in_specs, out_specs=out_specs, check_vma=False
    )
```

```python
import functools

import jax
import jax.numpy as jnp
from jax import lax
from jax.experimental import pallas as pl
from jax.experimental.pallas import tpu as pltpu
from jax.sharding import PartitionSpec as P

MESH = pl.DeviceIdType.MESH
F32, BF16 = jnp.float32, jnp.bfloat16
HOP_CHUNKS = 2
UNIT_CHUNKS = 3
GRAD_CHUNKS = 3
SWAP_BLOCKS = 4


def dot(a, b):
    return jnp.dot(a, b, preferred_element_type=F32)


def sigmoid(x):
    return 0.5 + 0.5 * jnp.tanh(0.5 * x)


def norm_factor(wide):
    return lax.rsqrt(jnp.mean(wide * wide, axis=-1, keepdims=True) + 1e-05)


def relay_kernel(
    S, DP, scale,
    feed, win, wout, oa, ob,
    wa, wb, wat, wbt, h_all, g_all, h_out, g_out, pre_own, dsl_own, hid_own, dpre_own, u_own, r_own,
    n_t, h_t, dsl_all, up_a, got_a, own_a, own_b, hm_t, fin_a, fin_b, end_a, end_b,
    dh_own, full_t,
    load_sem, feed_sem, swap_send, swap_recv, hop_send, hop_recv, all_send, all_recv,
    up_send, up_recv, pair_send, pair_recv, fin_send, fin_recv,
):
    s, d = lax.axis_index("section"), lax.axis_index("dp")
    M, D = h_all.shape[2], h_all.shape[3]
    R = wa.shape[2]
    T = DP * M
    ra, rb = D // DP, R // DP
    last = S // 2 - 1
    p = lax.rem(s, 2)
    place = s // 2 + p * (last - 2 * (s // 2))
    mate = s + 1 - 2 * p
    stride = 2 * (1 - 2 * p)
    mirror = S - 1 - s
    cw, uw, gw = D // HOP_CHUNKS, R // UNIT_CHUNKS, R // GRAD_CHUNKS

    def unit_cols(c):
        return pl.ds(pl.multiple_of(c * uw, uw), uw)

    def load(i):
        src, dst = ((win, wa), (wout, wb))[i]
        return pltpu.make_async_copy(src.at[p, 0], dst.at[0], load_sem.at[i])

    def remote(src, dst, send_sem, recv_sem, section):
        return pltpu.make_async_remote_copy(
            src_ref=src,
            dst_ref=dst,
            send_sem=send_sem,
            recv_sem=recv_sem,
            device_id={"section": section},
            device_id_type=MESH,
        )

    def swap(i, b):
        src, dst = ((win, wa), (wout, wb))[i]
        rows = pl.ds(b * (dst.shape[1] // SWAP_BLOCKS), dst.shape[1] // SWAP_BLOCKS)
        return remote(
            src.at[1 - p, 0, rows], dst.at[1, rows], swap_send.at[i, b], swap_recv.at[i, b], mate
        )

    def swap_wait(i):
        for b in range(SWAP_BLOCKS):
            swap(i, b).wait_recv()

    feed_copy = pltpu.make_async_copy(feed.at[p], h_all.at[0, d], feed_sem)

    @pl.when(place == 0)
    def _():
        feed_copy.start()

    load(0).start()
    load(1).start()

    barrier = pltpu.get_barrier_semaphore()
    for other in (mate, lax.rem(s + 2, S), lax.rem(s + S - 2, S), mirror):
        pl.semaphore_signal(barrier, inc=1, device_id={"section": other}, device_id_type=MESH)
    for o in range(1, DP):
        pl.semaphore_signal(
            barrier, inc=1, device_id={"dp": lax.rem(d + o, DP)}, device_id_type=MESH
        )
    pl.semaphore_wait(barrier, 4 + DP - 1)

    for i in range(2):
        for b in range(SWAP_BLOCKS):
            swap(i, b).start()

    def hop(kind, c):
        cols = pl.ds(c * cw, cw)
        src, dst = ((h_out, h_all.at[0, d]), (g_out, g_all.at[1, d]))[kind]
        peer = s + stride if kind == 0 else s - stride
        return remote(
            src.at[:, cols], dst.at[:, cols], hop_send.at[kind, c], hop_recv.at[kind, c], peer
        )

    def share(kind, i, o, incoming=False):
        buf = (h_all, g_all)[kind]
        peer = lax.rem(d + (DP - o if incoming else o), DP)
        block = buf.at[i, peer if incoming else d]
        return pltpu.make_async_remote_copy(
            src_ref=block,
            dst_ref=block,
            send_sem=all_send.at[kind, i, o - 1],
            recv_sem=all_recv.at[kind, i, o - 1],
            device_id={"dp": peer},
            device_id_type=MESH,
        )

    def share_start(kind, i):
        for o in range(1, DP):
            share(kind, i, o).start()

    def take_wait(kind, i):
        for o in range(1, DP):
            share(kind, i, o, True).wait_recv()

    def up_copy(i, c):
        cols = pl.ds(c * gw, gw)
        return remote(
            up_a.at[i, :, cols], got_a.at[i, :, cols], up_send.at[i, c], up_recv.at[i, c], mirror
        )

    def hidden_copy(i):
        return remote(h_t.at[i], hm_t.at[i], pair_send.at[0, i], pair_recv.at[0, i], mirror)

    def seed_copy(i):
        return remote(
            g_all.at[i, d], g_all.at[2 + i, d], pair_send.at[1, i], pair_recv.at[1, i], mirror
        )

    def final_copy(i):
        src, dst = ((fin_a, end_a), (fin_b, end_b))[i]
        return remote(src, dst, fin_send.at[i], fin_recv.at[i], mate)

    def forward(i):
        steps = HOP_CHUNKS if i == 0 else 1
        width = D // steps
        squares = jnp.zeros((M, 1), F32)
        for c in range(steps):
            part = pl.ds(c * width, width)
            if i == 0:

                @pl.when(place > 0)
                def _():
                    hop(0, c).wait_recv()

            piece = h_all[i, d, :, part]
            wide = piece.astype(F32)
            squares += jnp.sum(wide * wide, axis=-1, keepdims=True)
            end = c == steps - 1
            if end:
                factor = lax.rsqrt(squares * (1.0 / D) + 1e-05)
            for u in range(UNIT_CHUNKS):
                cols = pl.ds(u * uw, uw)
                before = dot(piece, wa[i, part, cols])
                if c:
                    before += pre_own[i, :, cols]
                if end:
                    before *= factor
                    hid_own[:, cols] = (before * sigmoid(before)).astype(BF16)
                pre_own[i, :, cols] = before

        @pl.when(place < last)
        def _():
            if i == 0:
                load(1).wait()
            else:
                swap_wait(1)

        for c in range(HOP_CHUNKS):
            cols = pl.ds(c * cw, cw)
            old = h_all[i, d, :, cols].astype(F32)
            new = (old + dot(hid_own[...], wb[i, :, cols])).astype(BF16)
            if i == 0:
                h_all[1, d, :, cols] = new
            else:
                h_out[:, cols] = new

                @pl.when(place < last)
                def _():
                    hop(0, c).start()

    def forward_rest(i):
        share_start(0, i)
        wide = h_all[i, d].astype(F32)
        factor = norm_factor(wide)
        u_own[i] = wide * factor
        r_own[i] = jnp.broadcast_to(factor, (M, 128))
        for u in range(UNIT_CHUNKS):
            cols = pl.ds(u * uw, uw)
            before = pre_own[i, :, cols]
            sigma = sigmoid(before)
            dsl_own[i, :, cols] = sigma * (1.0 + before * (1.0 - sigma))

    def spread(i):
        share_start(1, i)

        @pl.when(p == 1)
        def _():
            seed_copy(i).start()

    def backward(i):
        steps = HOP_CHUNKS if i == 1 else 1
        width = D // steps
        total = jnp.zeros((M, 1), F32)
        for c in range(steps):
            part = pl.ds(c * width, width)
            if i == 1:

                @pl.when(place < last)
                def _():
                    hop(1, c).wait_recv()

                if c == steps - 1:
                    spread(1)

            piece = g_all[i, d, :, part]
            for u in range(UNIT_CHUNKS):
                cols = pl.ds(u * uw, uw)
                d_hidden = dot(piece, wbt[i, part, cols])
                if c:
                    d_hidden += dh_own[:, cols]
                if c < steps - 1:
                    dh_own[:, cols] = d_hidden
                else:
                    d_before = (d_hidden * dsl_own[i, :, cols]).astype(BF16)
                    dpre_own[:, cols] = d_before
                    total += jnp.sum(
                        d_before.astype(F32) * pre_own[i, :, cols], axis=-1, keepdims=True
                    )
        mean = total * (1.0 / D)
        factor = r_own[i, :, 0:1]
        for c in range(HOP_CHUNKS):
            cols = pl.ds(c * cw, cw)
            d_normed = dot(dpre_own[...], wat[i, :, cols])
            out = g_all[i, d, :, cols].astype(F32) + factor * (
                d_normed - u_own[i, :, cols] * mean
            )
            if i == 1:
                g_all[0, d, :, cols] = out.astype(BF16)
            else:
                g_out[:, cols] = out.astype(BF16)
                hop(1, c).start()

    aligned = ra % 128 == 0 and rb % 128 == 0
    block = min(T, 256)

    def prepare(i):
        take_wait(0, i)

        def rows_step(b):
            per = block // M
            rows = pl.ds(pl.multiple_of(b * block, block), block)
            wide = h_all[i, pl.ds(b * per, per)].reshape(block, D).astype(F32)
            factor = norm_factor(wide)
            normed_wide = wide * factor
            normed = normed_wide.astype(BF16)
            if aligned:
                mine = h_all[
                    i, pl.ds(b * per, per), :, pl.ds(pl.multiple_of(d * ra, 128), ra)
                ].reshape(block, ra).astype(F32) * factor
                n_t[i, :, rows] = mine.T.astype(BF16)
                before = dot(normed, wa[i, :, pl.ds(pl.multiple_of(d * rb, 128), rb)])
                h_t[i, :, rows] = (before * sigmoid(before)).T.astype(BF16)
            else:
                full_t[0:D, rows] = normed_wide.T.astype(BF16)

            @pl.loop(0, UNIT_CHUNKS)
            def _(c):
                cols = unit_cols(c)
                before = dot(normed, wa[i, :, cols])
                sigma = sigmoid(before)
                dsl_all[i, rows, cols] = sigma * (1.0 + before * (1.0 - sigma))
                if not aligned:
                    full_t[pl.ds(pl.multiple_of(D + c * uw, 16), uw), rows] = (
                        (before * sigma).T.astype(BF16)
                    )

        if T == block:
            rows_step(0)
        else:
            pl.loop(0, T // block)(rows_step)
        if not aligned:
            n_t[i] = full_t[pl.ds(pl.multiple_of(d * ra, 16), ra), :]
            h_t[i] = full_t[pl.ds(pl.multiple_of(D + d * rb, 16), rb), :]

        @pl.when(p == 1)
        def _():
            hidden_copy(i).start()

    def gradients(i):
        take_wait(1, i)
        for c in range(GRAD_CHUNKS):
            cols = pl.ds(c * gw, gw)
            d_hidden = dot(g_all[i].reshape(T, D), wbt[i, :, cols])
            d_before = (d_hidden * dsl_all[i, :, cols]).astype(BF16)
            term = dot(n_t[i], d_before)

            @pl.when(p == 1)
            def _():
                up_a[i, :, cols] = term.astype(BF16)
                up_copy(i, c).start()

            @pl.when(p == 0)
            def _():
                own_a[i, :, cols] = term

        @pl.when(p == 0)
        def _():
            own_b[i] = dot(h_t[i], g_all[i].reshape(T, D))

    def finish(i, out_a, out_b):
        hidden_copy(i).wait_recv()
        take_wait(1, 2 + i)
        out_b[...] = (own_b[i] + dot(hm_t[i], g_all[2 + i].reshape(T, D))).astype(BF16)
        for c in range(GRAD_CHUNKS):
            cols = pl.ds(c * gw, gw)
            up_copy(i, c).wait_recv()
            out_a[:, cols] = (own_a[i, :, cols] + got_a[i, :, cols].astype(F32)).astype(BF16)

    def turn_weights():
        @pl.loop(0, 2)
        def _(i):
            @pl.loop(0, UNIT_CHUNKS)
            def _(c):
                cols = unit_cols(c)
                wbt[i, :, cols] = wb[i, cols, :].T
                wat[i, cols, :] = wa[i, :, cols].T

    load(0).wait()

    @pl.when(place == last)
    def _():
        load(1).wait()
        for i in range(2):
            swap_wait(i)
        turn_weights()

    @pl.when(place == 0)
    def _():
        feed_copy.wait()

    forward(0)

    @pl.when(place < last)
    def _():
        swap_wait(0)

    forward(1)

    @pl.when(place == last)
    def _():
        g_all[1, d] = (scale * h_out[...].astype(F32)).astype(BF16)

    for i in range(2):
        forward_rest(i)

    @pl.when(place < last)
    def _():
        turn_weights()
        pl.loop(0, 2)(prepare)

    backward(1)

    @pl.when(place > 0)
    def _():
        backward(0)

    spread(0)

    @pl.when(p == 0)
    def _():
        for i in (1, 0):
            seed_copy(i).wait_recv()
            share_start(1, 2 + i)

    @pl.when(place == last)
    def _():
        pl.loop(0, 2)(prepare)

    gradients(1)
    gradients(0)

    @pl.when(p == 0)
    def _():
        finish(1, fin_a, fin_b)
        final_copy(0).start()
        final_copy(1).start()
        finish(0, oa, ob)

    @pl.when(p == 1)
    def _():
        final_copy(0).wait_recv()
        oa[...] = end_a[...]
        final_copy(1).wait_recv()
        ob[...] = end_b[...]

    for i in range(2):
        for b in range(SWAP_BLOCKS):
            swap(i, b).wait_send()

    for kind, sent in ((0, place < last), (1, place > 0)):

        @pl.when(sent)
        def _():
            for c in range(HOP_CHUNKS):
                hop(kind, c).wait_send()

        for i in range(2):
            for o in range(1, DP):
                share(kind, i, o).wait_send()

    @pl.when(p == 0)
    def _():
        for i in range(2):
            final_copy(i).wait_send()
            for o in range(1, DP):
                share(1, 2 + i, o).wait_send()

    @pl.when(p == 1)
    def _():
        for i in range(2):
            hidden_copy(i).wait_send()
            seed_copy(i).wait_send()
            for c in range(GRAD_CHUNKS):
                up_copy(i, c).wait_send()


def widen_kernel(a_ref, b_ref, oa_ref, ob_ref):
    oa_ref[0] = a_ref[...].astype(F32)
    ob_ref[0] = b_ref[...].astype(F32)


def widen(a, b):
    parts = 2

    def narrow(x):
        return pl.BlockSpec((x.shape[0], x.shape[1] // parts), lambda i: (0, i))

    def wide(x):
        return pl.BlockSpec((1, x.shape[0], x.shape[1] // parts), lambda i: (0, 0, i))

    return pl.pallas_call(
        widen_kernel,
        grid=(parts,),
        out_shape=tuple(jax.ShapeDtypeStruct((1,) + x.shape, F32) for x in (a, b)),
        in_specs=[narrow(a), narrow(b)],
        out_specs=(wide(a), wide(b)),
        compiler_params=pltpu.CompilerParams(vmem_limit_bytes=60 * 1024 * 1024),
        cost_estimate=pl.CostEstimate(
            flops=a.size + b.size, bytes_accessed=6 * (a.size + b.size), transcendentals=0
        ),
    )(a, b)


def per_device(feed, proj_in, proj_out):
    S, DP = lax.axis_size("section"), lax.axis_size("dp")
    micro, rows, D = feed.shape[1:]
    R = proj_in.shape[3]
    M, T = micro * rows, micro * rows * DP
    ra, rb = D // DP, R // DP
    scale = 8.0 / T
    aligned = ra % 128 == 0 and rb % 128 == 0
    vm = pltpu.VMEM
    dma = pltpu.SemaphoreType.DMA
    peers = max(DP - 1, 1)
    grad_a, grad_b = pl.pallas_call(
        functools.partial(relay_kernel, S, DP, scale),
        out_shape=(
            jax.ShapeDtypeStruct((ra, R), BF16),
            jax.ShapeDtypeStruct((rb, D), BF16),
        ),
        in_specs=[pl.BlockSpec(memory_space=pltpu.HBM)] * 3,
        out_specs=(pl.BlockSpec(memory_space=pltpu.VMEM),) * 2,
        scratch_shapes=[
            vm((2, D, R), BF16),
            vm((2, R, D), BF16),
            vm((2, R, D), BF16),
            vm((2, D, R), BF16),
            vm((2, DP, M, D), BF16),
            vm((4, DP, M, D), BF16),
            vm((M, D), BF16),
            vm((M, D), BF16),
            vm((2, M, R), F32),
            vm((2, M, R), F32),
            vm((M, R), BF16),
            vm((M, R), BF16),
            vm((2, M, D), F32),
            vm((2, M, 128), F32),
            vm((2, ra, T), BF16),
            vm((2, rb, T), BF16),
            vm((2, T, R), F32),
            vm((2, ra, R), BF16),
            vm((2, ra, R), BF16),
            vm((2, ra, R), F32),
            vm((2, rb, D), F32),
            vm((2, rb, T), BF16),
            vm((ra, R), BF16),
            vm((rb, D), BF16),
            vm((ra, R), BF16),
            vm((rb, D), BF16),
            vm((M, R), F32),
            vm((16, 128) if aligned else (D + R, T), BF16),
            dma((2,)),
            dma(()),
            dma((2, SWAP_BLOCKS)),
            dma((2, SWAP_BLOCKS)),
            dma((2, HOP_CHUNKS)),
            dma((2, HOP_CHUNKS)),
            dma((2, 4, peers)),
            dma((2, 4, peers)),
            dma((2, GRAD_CHUNKS)),
            dma((2, GRAD_CHUNKS)),
            dma((2, 2)),
            dma((2, 2)),
            dma((2,)),
            dma((2,)),
        ],
        compiler_params=pltpu.CompilerParams(
            collective_id=0, has_side_effects=True, vmem_limit_bytes=60 * 1024 * 1024
        ),
        cost_estimate=pl.CostEstimate(
            flops=40 * M * D * R, bytes_accessed=16 * D * R, transcendentals=8 * T * R
        ),
    )(feed.reshape(2, M, D), proj_in, proj_out)
    return widen(grad_a, grad_b)


def solution(mesh):
    in_specs = (
        P(None, None, "dp", None),
        P(None, "section", None, None),
        P(None, "section", None, None),
    )
    out_specs = (P("section", "dp", None), P("section", "dp", None))
    return jax.shard_map(
        per_device, mesh=mesh, in_specs=in_specs, out_specs=out_specs, check_vma=False
    )
```
